128 devices in a mesh: scene: 8 (over y, core), frame: 16 (over z, x).
Axes of the slice: x: 4, y: 4, z: 4, core: 2. Of those that a mesh axis runs over, the one named last changes fastest.
Arguments:
- occupancy: bfloat16 [8, 64, 64, 2048], P('scene', 'frame'), may hold values from -6 to 6
- scene_lengths: int32 [8], P('scene'), may hold values from 8 to 64, as said below
- conv1_weight: bfloat16 [128, 1728], replicated, may hold values from -0.15625 to 0.15625
- conv2_weight: bfloat16 [256, 3456], replicated, may hold values from -0.109375 to 0.109375
- temporal_weight: bfloat16 [3, 256, 256], replicated, may hold values from -0.21875 to 0.21875
- query_weight: bfloat16 [256, 256], replicated
- key_weight: bfloat16 [256, 256], replicated
- value_weight: bfloat16 [256, 256], replicated, may hold values from -0.375 to 0.375
- out_weight: bfloat16 [256, 256], replicated, may hold values from -0.375 to 0.375
Outputs:
- encoded: bfloat16 [8, 64, 256, 512], P('scene', 'frame')
- kl_loss: float32 [], replicated
The draws below stay inside these ranges and needn't reach their ends.
Inputs may be any that keep to these rules, and one draw needn't show every extreme that they name: `scene_lengths`: non-decreasing along the scenes; the first scene has exactly 8 frames with data and the last exactly 64.
All inputs are finite; a program needn't handle non-finite values.
Results may differ from the reference program's by a relative error of at most 0.011.
Values may be sent and summed in bfloat16 or wider, within the bound.
A program may use at most 192 MiB of HBM per device.

```python
import jax
import jax.numpy as jnp
from jax import lax

CIN = 64
C1 = 128
C2 = 256
HEADS = 4
HD = 64
HI = 16
ZD = 8
CELLS = 512
CELLS_IN = 2048
FRAMES = 64
SCENES = 8


def query_key_pair(key):
    base_key = jax.random.fold_in(key, 11)
    first_draw = jax.random.normal(jax.random.fold_in(base_key, 1), (C2, C2), jnp.float32) * C2 ** (-0.5)
    second_draw = jax.random.normal(jax.random.fold_in(base_key, 2), (C2, C2), jnp.float32) * C2 ** (-0.5)
    return (first_draw, second_draw)


def draw_query_weight(key, part):
    first_draw, second_draw = query_key_pair(key)
    return first_draw.astype(jnp.bfloat16)


def draw_key_weight(key, part):
    first_draw, second_draw = query_key_pair(key)
    return second_draw.astype(jnp.bfloat16)


def draw_scene_lengths(key, part):
    drawn = jax.random.randint(jax.random.fold_in(key, 3), (SCENES,), 8, FRAMES + 1)
    drawn = jnp.sort(drawn)
    drawn = drawn.at[0].set(8)
    drawn = drawn.at[SCENES - 1].set(FRAMES)
    return drawn.astype(jnp.int32)


def level_of(key, extent, cuts, low, top_value):
    def one(position, blocks):
        steps = jax.random.uniform(jax.random.fold_in(jax.random.fold_in(key, 6), position), (blocks,), jnp.float32, low / len(cuts), top_value / len(cuts))
        return jnp.repeat(jnp.exp(steps), extent[position] // blocks).reshape((-1,) + (1,) * (len(extent) - position - 1))

    factor_of = one(*cuts[0])
    for cut in cuts[1:]:
        factor_of = factor_of * one(*cut)
    return factor_of


def centred(key, dims, scale, reach, shards=(), kind=jnp.bfloat16):
    loudness = level_of(key, dims, shards, -0.22, 0.18) if shards else 1.0
    values = jax.random.normal(key, dims, jnp.float32) * scale * loudness
    return jnp.minimum(jnp.maximum(values, -reach), reach).astype(kind)


def setup_inputs(seed: int = 0) -> dict:
    key_of = jax.random.split(jax.random.key(seed), 10)
    occupancy = centred(key_of[0], (SCENES, FRAMES, CIN, CELLS_IN), 1.0, 6.0, ((0, 8), (1, 16)))
    scene_lengths = draw_scene_lengths(jax.random.fold_in(key_of[9], 71), 0)
    conv1_weight = centred(key_of[2], (C1, CIN * 27), (CIN * 27) ** -0.5, 0.15625)
    conv2_weight = centred(key_of[3], (C2, C1 * 27), (C1 * 27) ** -0.5, 0.109375)
    temporal_weight = centred(key_of[4], (3, C2, C2), (3 * C2) ** -0.5, 0.21875)
    query_weight = draw_query_weight(jax.random.fold_in(key_of[9], 71), 0)
    key_weight = draw_key_weight(jax.random.fold_in(key_of[9], 71), 0)
    value_weight = centred(key_of[7], (C2, C2), C2 ** -0.5, 0.375)
    out_weight = centred(key_of[8], (C2, C2), C2 ** -0.5, 0.375)
    return {"occupancy": occupancy, "scene_lengths": scene_lengths, "conv1_weight": conv1_weight, "conv2_weight": conv2_weight, "temporal_weight": temporal_weight, "query_weight": query_weight, "key_weight": key_weight, "value_weight": value_weight, "out_weight": out_weight}


NORM_EPS = 1e-06

def spatial_conv(voxels, weight, channels_in, stride):
    channels_out = weight.shape[0]
    kernel = weight.reshape(channels_out, channels_in, 3, 3, 3)
    return lax.conv_general_dilated(voxels, kernel, (stride, stride, 1), ((1, 1), (1, 1), (1, 1)), dimension_numbers=('NCDHW', 'OIDHW', 'NCDHW'), preferred_element_type=jnp.float32)

def mix_channels(weight, maps):
    return jnp.einsum('oc,fcn->fon', weight.astype(jnp.float32), maps.astype(jnp.float32))

def encode_scene(occupancy, length, conv1_weight, conv2_weight, temporal_weight, query_weight, key_weight, value_weight, out_weight):
    frames = occupancy.shape[0]
    voxels = occupancy.reshape(frames, CIN, HI, HI, ZD)
    first_maps = jax.nn.silu(spatial_conv(voxels, conv1_weight, CIN, 2)).astype(jnp.bfloat16)
    second_full = jax.nn.silu(spatial_conv(first_maps, conv2_weight, C1, 1))
    valid_rows = (jnp.arange(frames) < length).astype(jnp.float32)
    second_maps = (second_full.reshape(frames, C2, CELLS) * valid_rows[:, None, None]).astype(jnp.bfloat16)
    padded = jnp.pad(second_maps, ((1, 1), (0, 0), (0, 0)))
    temporal_sum = mix_channels(temporal_weight[0], padded[0:frames])
    temporal_sum = temporal_sum + mix_channels(temporal_weight[1], padded[1:frames + 1])
    temporal_sum = temporal_sum + mix_channels(temporal_weight[2], padded[2:frames + 2])
    residual_maps = (second_maps.astype(jnp.float32) + jax.nn.silu(temporal_sum)).astype(jnp.bfloat16)
    residual_f = residual_maps.astype(jnp.float32)
    normed = (residual_f * lax.rsqrt(lax.optimization_barrier(jnp.mean(residual_f * residual_f, axis=1, keepdims=True)) + NORM_EPS)).astype(jnp.bfloat16)
    queries = mix_channels(query_weight, normed).astype(jnp.bfloat16).reshape(frames, HEADS, HD, CELLS)
    key_rows = mix_channels(key_weight, normed).astype(jnp.bfloat16).reshape(frames, HEADS, HD, CELLS)
    value_rows = mix_channels(value_weight, normed).astype(jnp.bfloat16).reshape(frames, HEADS, HD, CELLS)
    scores = jnp.einsum('qhdc,khdc->qkhc', queries.astype(jnp.float32), key_rows.astype(jnp.float32)) * HD ** (-0.5)
    key_mask = (jnp.arange(frames) < length)[None, :, None, None]
    scores = jnp.where(key_mask, scores, -1e+30)
    row_max = lax.optimization_barrier(jnp.max(scores, axis=1, keepdims=True))
    raw_weights = jnp.where(key_mask, jnp.exp(scores - row_max), 0.0)
    row_total = lax.optimization_barrier(jnp.sum(raw_weights, axis=1))
    exp_weights = lax.optimization_barrier(raw_weights.astype(jnp.bfloat16))
    weighted = jnp.einsum('qkhc,khdc->qhdc', exp_weights.astype(jnp.float32), value_rows.astype(jnp.float32))
    attended = (weighted / row_total[:, :, None, :]).astype(jnp.bfloat16)
    out_full = residual_f + mix_channels(out_weight, attended.reshape(frames, C2, CELLS))
    return (out_full * valid_rows[:, None, None]).astype(jnp.bfloat16)

def reference(occupancy, scene_lengths, conv1_weight, conv2_weight, temporal_weight, query_weight, key_weight, value_weight, out_weight):

    def one_scene(pair_in):
        return encode_scene(pair_in[0], pair_in[1], conv1_weight, conv2_weight, temporal_weight, query_weight, key_weight, value_weight, out_weight)
    encoded = lax.map(one_scene, (occupancy, scene_lengths))
    grand_total = jnp.sum(jnp.square(encoded.astype(jnp.float32)))
    kl_loss = 0.5 * grand_total / float(SCENES * FRAMES * CELLS * C2)
    return (encoded, kl_loss)
```

```python
import jax
import jax.numpy as jnp
from jax import lax
from jax.sharding import PartitionSpec as P

CIN = 64
C1 = 128
C2 = 256
HEADS = 4
HD = 64
HI = 16
ZD = 8
CELLS = 512


NORM_EPS = 1e-06


def spatial_conv(voxels, weight, channels_in, stride):
    channels_out = weight.shape[0]
    kernel = weight.reshape(channels_out, channels_in, 3, 3, 3)
    return lax.conv_general_dilated(
        voxels,
        kernel,
        (stride, stride, 1),
        ((1, 1), (1, 1), (1, 1)),
        dimension_numbers=("NCDHW", "OIDHW", "NCDHW"),
        preferred_element_type=jnp.float32,
    )


def mix(maps, weight):
    return jnp.einsum("tnc,oc->tno", maps, weight, preferred_element_type=jnp.float32)


def shards(
    occupancy,
    scene_lengths,
    conv1_weight,
    conv2_weight,
    temporal_weight,
    query_weight,
    key_weight,
    value_weight,
    out_weight,
):
    f_dev = occupancy.shape[1]
    length = scene_lengths[0]
    first_frame = lax.axis_index("frame") * f_dev
    frame_ids = first_frame + jnp.arange(f_dev, dtype=jnp.int32)
    valid_rows = (frame_ids < length).astype(jnp.float32)
    voxels = occupancy[0].reshape(f_dev, CIN, HI, HI, ZD)
    first_maps = jax.nn.silu(spatial_conv(voxels, conv1_weight, CIN, 2)).astype(jnp.bfloat16)
    second_full = jax.nn.silu(spatial_conv(first_maps, conv2_weight, C1, 1))
    second_maps = (second_full.reshape(f_dev, C2, CELLS) * valid_rows[:, None, None]).astype(
        jnp.bfloat16
    )
    second = lax.all_to_all(second_maps.transpose(0, 2, 1), "frame", 1, 0, tiled=True)
    frames, cells = second.shape[:2]
    padded = jnp.pad(second, ((1, 1), (0, 0), (0, 0)))
    temporal_sum = mix(padded[0:frames], temporal_weight[0])
    for tap in range(1, 3):
        temporal_sum = temporal_sum + mix(padded[tap : tap + frames], temporal_weight[tap])
    residual = (second.astype(jnp.float32) + jax.nn.silu(temporal_sum)).astype(jnp.bfloat16)
    residual = residual.astype(jnp.float32)
    normed = (
        residual * lax.rsqrt(jnp.mean(residual * residual, axis=2, keepdims=True) + NORM_EPS)
    ).astype(jnp.bfloat16)
    split = (frames, cells, HEADS, HD)
    queries = mix(normed, query_weight).astype(jnp.bfloat16).reshape(split)
    keys = mix(normed, key_weight).astype(jnp.bfloat16).reshape(split)
    values = mix(normed, value_weight).astype(jnp.bfloat16).reshape(split)
    scores = jnp.einsum(
        "qnhd,knhd->nhqk", queries, keys, preferred_element_type=jnp.float32
    ) * HD ** (-0.5)
    key_mask = (jnp.arange(frames) < length)[None, None, None, :]
    scores = jnp.where(key_mask, scores, -1e30)
    row_max = jnp.max(scores, axis=3, keepdims=True)
    weights = jnp.where(key_mask, jnp.exp(scores - row_max), 0.0)
    total = jnp.sum(weights, axis=3, keepdims=True)
    weighted = jnp.einsum(
        "nhqk,knhd->nhqd",
        weights.astype(jnp.bfloat16),
        values,
        preferred_element_type=jnp.float32,
    )
    attended = (weighted / total).astype(jnp.bfloat16)
    attended = attended.transpose(2, 0, 1, 3).reshape(frames, cells, C2)
    row_valid = (jnp.arange(frames) < length).astype(jnp.float32)[:, None, None]
    encoded = ((residual + mix(attended, out_weight)) * row_valid).astype(jnp.bfloat16)
    squares = jnp.sum(jnp.square(encoded.astype(jnp.float32)))
    grand_total = lax.psum(squares, ("scene", "frame"))
    slot_count = float(lax.axis_size("scene") * frames * CELLS * C2)
    kl_loss = 0.5 * grand_total / slot_count
    encoded = lax.all_to_all(encoded, "frame", 0, 1, tiled=True).transpose(0, 2, 1)
    return (encoded[None], kl_loss)


def solution(mesh):
    placed = (P("scene", "frame", None, None), P("scene"), P(), P(), P(), P(), P(), P(), P())
    return jax.shard_map(
        shards,
        mesh=mesh,
        in_specs=placed,
        out_specs=(P("scene", "frame", None, None), P()),
        check_vma=False,
    )
```

```python
import functools

import jax
import jax.numpy as jnp
from jax import lax
from jax.experimental import pallas as pl
from jax.experimental.pallas import tpu as pltpu
from jax.sharding import PartitionSpec as P

CIN = 64
C1 = 128
C2 = 256
HEADS = 4
HD = 64
HI = 16
ZD = 8
CELLS = 512


NORM_EPS = 1e-06


def spatial_conv(voxels, weight, channels_in, stride):
    channels_out = weight.shape[0]
    kernel = weight.reshape(channels_out, channels_in, 3, 3, 3)
    return lax.conv_general_dilated(
        voxels,
        kernel,
        (stride, stride, 1),
        ((1, 1), (1, 1), (1, 1)),
        dimension_numbers=("NCDHW", "OIDHW", "NCDHW"),
        preferred_element_type=jnp.float32,
    )


FRAMES = 64
CHUNKS = 2
LOG2_E = 1.4426950408889634


def by_rows(rows, weight):
    return lax.dot_general(
        rows, weight, (((1,), (1,)), ((), ())), preferred_element_type=jnp.float32
    )


def silu(v):
    return v / (1.0 + jnp.exp(-v))


def mixing_kernel(
    count,
    scenes,
    length_ref,
    second_ref,
    temporal_ref,
    query_ref,
    key_ref,
    value_ref,
    out_weight_ref,
    encoded_ref,
    loss_ref,
    gathered,
    residual,
    q_rows,
    k_rows,
    v_rows,
    att_rows,
    done_rows,
    returned,
    total,
    frame_sums,
    scene_sums,
    there_send,
    there_recv,
    back_send,
    back_recv,
    frame_send,
    frame_recv,
    scene_send,
    scene_recv,
):
    f_dev = second_ref.shape[0]
    cells = CELLS // count
    part = cells // CHUNKS
    rows = FRAMES * part
    me = lax.axis_index("frame")
    my_scene = lax.axis_index("scene")
    length = length_ref[0]

    barrier = pltpu.get_barrier_semaphore()

    def greet_frame(d, carry):
        pl.semaphore_signal(
            barrier,
            inc=1,
            device_id={"frame": lax.rem(me + d, count)},
            device_id_type=pl.DeviceIdType.MESH,
        )
        return carry

    def greet_scene(d, carry):
        pl.semaphore_signal(
            barrier,
            inc=1,
            device_id={"scene": lax.rem(my_scene + d, scenes)},
            device_id_type=pl.DeviceIdType.MESH,
        )
        return carry

    lax.fori_loop(1, count, greet_frame, 0)
    lax.fori_loop(1, scenes, greet_scene, 0)
    pl.semaphore_wait(barrier, count - 1 + scenes - 1)

    def cells_of(device, chunk):
        return pl.ds(pl.multiple_of(device * cells + chunk * part, part), part)

    def there(chunk, d):
        to = lax.rem(me + d, count)
        return pltpu.make_async_remote_copy(
            src_ref=second_ref.at[:, cells_of(to, chunk), :],
            dst_ref=gathered.at[chunk, pl.ds(1 + f_dev * me, f_dev)],
            send_sem=there_send.at[chunk, d],
            recv_sem=there_recv.at[chunk, d],
            device_id={"frame": to},
            device_id_type=pl.DeviceIdType.MESH,
        )

    def back(chunk, d):
        to = lax.rem(me + d, count)
        return pltpu.make_async_remote_copy(
            src_ref=done_rows.at[chunk, pl.ds(f_dev * to, f_dev)],
            dst_ref=returned.at[:, cells_of(me, chunk), :],
            send_sem=back_send.at[chunk, d],
            recv_sem=back_recv.at[chunk, d],
            device_id={"frame": to},
            device_id_type=pl.DeviceIdType.MESH,
        )

    def frame_sum(d):
        return pltpu.make_async_remote_copy(
            src_ref=total,
            dst_ref=frame_sums.at[me],
            send_sem=frame_send.at[d],
            recv_sem=frame_recv.at[d],
            device_id={"frame": lax.rem(me + d, count)},
            device_id_type=pl.DeviceIdType.MESH,
        )

    def scene_sum(d):
        return pltpu.make_async_remote_copy(
            src_ref=total,
            dst_ref=scene_sums.at[my_scene],
            send_sem=scene_send.at[d],
            recv_sem=scene_recv.at[d],
            device_id={"scene": lax.rem(my_scene + d, scenes)},
            device_id_type=pl.DeviceIdType.MESH,
        )

    def each(first, last, act):
        def step(d, carry):
            act(d)
            return carry

        lax.fori_loop(first, last, step, 0)

    for chunk in range(CHUNKS):
        each(1, count, lambda d, chunk=chunk: there(chunk, d).start())
    for chunk in range(CHUNKS):
        gathered[chunk, 0] = jnp.zeros((part, C2), jnp.bfloat16)
        gathered[chunk, FRAMES + 1] = jnp.zeros((part, C2), jnp.bfloat16)
        gathered[chunk, pl.ds(1 + f_dev * me, f_dev)] = second_ref[:, cells_of(me, chunk), :]

    span = 256 // part
    block = span * part
    head_of = lax.broadcasted_iota(jnp.int32, (FRAMES, C2), 1) // HD
    ones4 = (
        lax.broadcasted_iota(jnp.int32, (C2, C2), 0) // HD
        == lax.broadcasted_iota(jnp.int32, (C2, C2), 1) // HD
    ).astype(jnp.bfloat16)
    key_mask = lax.broadcasted_iota(jnp.int32, (FRAMES, C2), 1) % FRAMES < length
    low_half = lax.broadcasted_iota(jnp.int32, (FRAMES, 128), 1) < HD
    total[...] = jnp.zeros_like(total)

    for chunk in range(CHUNKS):
        each(1, count, lambda d, chunk=chunk: there(chunk, d).wait_recv())

        def project(b, carry, chunk=chunk):
            window = gathered[chunk, pl.ds(b * span, span + 2)].reshape((span + 2) * part, C2)
            temporal = by_rows(window[:block], temporal_ref[0])
            temporal = temporal + by_rows(window[part : part + block], temporal_ref[1])
            temporal = temporal + by_rows(window[2 * part :], temporal_ref[2])
            here = window[part : part + block].astype(jnp.float32)
            mixed = (here + silu(temporal)).astype(jnp.bfloat16)
            at = pl.ds(pl.multiple_of(b * block, block), block)
            residual[at, :] = mixed
            wide = mixed.astype(jnp.float32)
            scale = lax.rsqrt(jnp.mean(wide * wide, axis=1, keepdims=True) + NORM_EPS)
            normed = (wide * scale).astype(jnp.bfloat16)
            for weight_ref, into in ((query_ref, q_rows), (key_ref, k_rows), (value_ref, v_rows)):
                made = by_rows(normed, weight_ref[...])
                into[0, at, :] = made[:, :128]
                into[1, at, :] = made[:, 128:]
            return carry

        lax.fori_loop(0, FRAMES // span, project, 0)

        def cell_rows(ref, cell):
            at = pl.ds(cell, FRAMES, stride=part)
            return jnp.concatenate([ref[0, at, :], ref[1, at, :]], axis=1).astype(jnp.bfloat16)

        def spread(found):
            zero = jnp.zeros_like(found)
            return jnp.concatenate([jnp.where(head_of == h, found, zero) for h in range(HEADS)], 0)

        def attend(cell, carry):
            queries = cell_rows(q_rows, cell)
            keys = spread(cell_rows(k_rows, cell))
            values = spread(cell_rows(v_rows, cell))
            scores = jnp.where(key_mask, by_rows(queries, keys), -1e30)
            tops = []
            for half in range(2):
                piece = scores[:, half * 128 : half * 128 + 128]
                low = jnp.max(jnp.where(low_half, piece, -1e30), axis=1, keepdims=True)
                high = jnp.max(jnp.where(low_half, -1e30, piece), axis=1, keepdims=True)
                tops.append(jnp.where(low_half, low, high))
            top = jnp.concatenate(tops, axis=1)
            weights = jnp.exp2((scores - top) * (LOG2_E * HD**-0.5)).astype(jnp.bfloat16)
            weighted = jnp.dot(weights, values, preferred_element_type=jnp.float32)
            sums = jnp.dot(weights, ones4, preferred_element_type=jnp.float32)
            attended = weighted / sums
            at = pl.ds(cell, FRAMES, stride=part)
            att_rows[0, at, :] = attended[:, :128]
            att_rows[1, at, :] = attended[:, 128:]
            return carry

        lax.fori_loop(0, part, attend, 0)

        def finish(b, carry, chunk=chunk):
            at = pl.ds(pl.multiple_of(b * block, block), block)
            attended = jnp.concatenate([att_rows[0, at, :], att_rows[1, at, :]], axis=1)
            full = residual[at, :].astype(jnp.float32) + by_rows(
                attended.astype(jnp.bfloat16), out_weight_ref[...]
            )
            frame = b * span + lax.broadcasted_iota(jnp.int32, (block, C2), 0) // part
            kept = jnp.where(frame < length, full, 0.0).astype(jnp.bfloat16)
            done_rows[chunk, pl.ds(b * span, span)] = kept.reshape(span, part, C2)
            wide = kept.astype(jnp.float32)
            squares = jnp.sum((wide * wide).reshape(block // 8, 8, C2), axis=0)
            total[...] += squares[:, :128] + squares[:, 128:]
            return carry

        lax.fori_loop(0, FRAMES // span, finish, 0)
        each(1, count, lambda d, chunk=chunk: back(chunk, d).start())
        returned[:, cells_of(me, chunk), :] = done_rows[chunk, pl.ds(f_dev * me, f_dev)]

    each(1, count, lambda d: frame_sum(d).start())
    frame_sums[me] = total[...]
    each(1, count, lambda d: frame_sum(d).wait_recv())
    each(1, count, lambda d: frame_sum(d).wait_send())
    total[...] = jnp.sum(frame_sums[...], axis=0)
    each(1, scenes, lambda d: scene_sum(d).start())
    scene_sums[my_scene] = total[...]

    eye = (
        lax.broadcasted_iota(jnp.int32, (C2, C2), 0)
        == lax.broadcasted_iota(jnp.int32, (C2, C2), 1)
    ).astype(jnp.bfloat16)
    for chunk in range(CHUNKS):
        each(1, count, lambda d, chunk=chunk: back(chunk, d).wait_recv())

    def turn(f, carry):
        encoded_ref[f] = by_rows(eye, returned[f]).astype(jnp.bfloat16)
        return carry

    lax.fori_loop(0, f_dev, turn, 0)

    each(1, scenes, lambda d: scene_sum(d).wait_recv())
    loss_ref[...] = jnp.sum(scene_sums[...], axis=0)
    each(1, scenes, lambda d: scene_sum(d).wait_send())
    for chunk in range(CHUNKS):
        each(1, count, lambda d, chunk=chunk: there(chunk, d).wait_send())
        each(1, count, lambda d, chunk=chunk: back(chunk, d).wait_send())


def shards(
    occupancy,
    scene_lengths,
    conv1_weight,
    conv2_weight,
    temporal_weight,
    query_weight,
    key_weight,
    value_weight,
    out_weight,
):
    f_dev = occupancy.shape[1]
    length = scene_lengths[0]
    count, scenes = lax.axis_size("frame"), lax.axis_size("scene")
    first_frame = lax.axis_index("frame") * f_dev
    frame_ids = first_frame + jnp.arange(f_dev, dtype=jnp.int32)
    valid_rows = (frame_ids < length).astype(jnp.float32)
    voxels = occupancy[0].reshape(f_dev, CIN, HI, HI, ZD)
    first_maps = jax.nn.silu(spatial_conv(voxels, conv1_weight, CIN, 2)).astype(jnp.bfloat16)
    second_full = jax.nn.silu(spatial_conv(first_maps, conv2_weight, C1, 1))
    second_maps = (second_full.reshape(f_dev, C2, CELLS) * valid_rows[:, None, None]).astype(
        jnp.bfloat16
    )
    second = second_maps.transpose(0, 2, 1)

    part = CELLS // count // CHUNKS
    rows = FRAMES * part
    wide_rows = pltpu.VMEM((2, rows, 128), jnp.float32)
    in_vmem = pl.BlockSpec(memory_space=pltpu.VMEM)
    encoded, sums = pl.pallas_call(
        functools.partial(mixing_kernel, count, scenes),
        out_shape=(
            jax.ShapeDtypeStruct((f_dev, C2, CELLS), jnp.bfloat16),
            jax.ShapeDtypeStruct((8, 128), jnp.float32),
        ),
        in_specs=[pl.BlockSpec(memory_space=pltpu.SMEM)] + [in_vmem] * 6,
        out_specs=(in_vmem, in_vmem),
        scratch_shapes=[
            pltpu.VMEM((CHUNKS, FRAMES + 2, part, C2), jnp.bfloat16),
            pltpu.VMEM((rows, C2), jnp.bfloat16),
            wide_rows,
            wide_rows,
            wide_rows,
            wide_rows,
            pltpu.VMEM((CHUNKS, FRAMES, part, C2), jnp.bfloat16),
            pltpu.VMEM((f_dev, CELLS, C2), jnp.bfloat16),
            pltpu.VMEM((8, 128), jnp.float32),
            pltpu.VMEM((count, 8, 128), jnp.float32),
            pltpu.VMEM((scenes, 8, 128), jnp.float32),
        ]
        + [pltpu.SemaphoreType.DMA((CHUNKS, count))] * 4
        + [pltpu.SemaphoreType.DMA((count,))] * 2
        + [pltpu.SemaphoreType.DMA((scenes,))] * 2,
        compiler_params=pltpu.CompilerParams(
            collective_id=0, has_side_effects=True, vmem_limit_bytes=48 * 2**20
        ),
    )(scene_lengths, second, temporal_weight, query_weight, key_weight, value_weight, out_weight)
    slot_count = float(scenes * FRAMES * CELLS * C2)
    kl_loss = 0.5 * jnp.sum(sums) / slot_count
    return (encoded[None], kl_loss)


def solution(mesh):
    placed = (P("scene", "frame", None, None), P("scene"), P(), P(), P(), P(), P(), P(), P())
    return jax.shard_map(
        shards,
        mesh=mesh,
        in_specs=placed,
        out_specs=(P("scene", "frame", None, None), P()),
        check_vma=False,
    )
```

```python
import functools

import jax
import jax.numpy as jnp
import numpy as np
from jax import lax
from jax.experimental import pallas as pl
from jax.experimental.pallas import tpu as pltpu
from jax.sharding import PartitionSpec as P

CIN = 64
C1 = 128
C2 = 256
HEADS = 4
HD = 64
HI = 16
ZD = 8
CELLS = 512


NORM_EPS = 1e-06


FRAMES = 64
CHUNKS = 2
LOG2_E = 1.4426950408889634


def by_rows(rows, weight):
    return lax.dot_general(
        rows, weight, (((1,), (1,)), ((), ())), preferred_element_type=jnp.float32
    )


def by_columns(rows, matrix):
    return jnp.dot(rows, matrix, preferred_element_type=jnp.float32)


def silu(v):
    return 0.5 * v * (1.0 + jnp.tanh(0.5 * v))


def picks_strided():
    picks = np.zeros((5, 8, ZD, 2, HI, ZD), np.float32)
    for tap in range(9):
        for out_y in range(8):
            for out_z in range(ZD):
                y, z = 2 * out_y + tap // 3 - 1, out_z + tap % 3 - 1
                if 0 <= y < HI and 0 <= z < ZD:
                    picks[tap // 2, out_y, out_z, tap % 2, y, z] = 1
    return picks.reshape(5 * 64, 2 * HI * ZD)


def picks_near():
    picks = np.zeros((9, 8, ZD, 8, ZD), np.float32)
    for tap in range(9):
        for out_y in range(8):
            for out_z in range(ZD):
                y, z = out_y + tap // 3 - 1, out_z + tap % 3 - 1
                if 0 <= y < 8 and 0 <= z < ZD:
                    picks[tap, out_y, out_z, y, z] = 1
    return picks.reshape(9 * 64, 64)


def order_weights(conv1_ref, conv2_ref, tall1, tall2, taps1, taps2):
    eye = (
        lax.broadcasted_iota(jnp.int32, (128, 128), 0)
        == lax.broadcasted_iota(jnp.int32, (128, 128), 1)
    ).astype(jnp.bfloat16)
    tall1[...] = conv1_ref[...].astype(jnp.float32)
    for at in range(0, C1 * 27, 128):
        turned = by_rows(eye, conv2_ref[:, at : at + 128])
        tall2[0, at : at + 128, :] = turned[:, :128]
        tall2[1, at : at + 128, :] = turned[:, 128:]
    for dx in range(3):
        for tap in range(9):
            at = pl.ds(dx * 9 + tap, CIN, stride=27)
            taps1[dx, tap * CIN : (tap + 1) * CIN, :] = tall1[at, :].astype(jnp.bfloat16)
            at = pl.ds(dx * 9 + tap, C1, stride=27)
            taps2[dx, tap * C1 : (tap + 1) * C1, :] = jnp.concatenate(
                [tall2[0, at, :], tall2[1, at, :]], axis=1
            ).astype(jnp.bfloat16)
        taps1[dx, 9 * CIN :, :] = jnp.zeros((CIN, C1), jnp.bfloat16)


def convolve_pair(
    pair, first_frame, length, occupancy_ref, picks1, picks2, taps1, taps2, even, odd, maps, near, second
):
    blank = jnp.zeros((CIN, 128), jnp.bfloat16)
    for x in range(HI):
        pieces = []
        for f in range(2):
            plane = occupancy_ref[2 * pair + f, :, x * 128 : (x + 1) * 128]
            pieces.append(jnp.concatenate([plane, blank], axis=1))
            pieces.append(jnp.concatenate([blank, plane], axis=1))
        found = by_rows(picks1[...], jnp.concatenate(pieces, axis=0)).astype(jnp.bfloat16)
        into, row = (even, x // 2) if x % 2 == 0 else (odd, x // 2 + 1)
        for f in range(2):
            for k in range(5):
                into[f, row, :, k * 128 : (k + 1) * 128] = found[
                    k * 64 : (k + 1) * 64, f * 128 : (f + 1) * 128
                ]
    for f in range(2):
        total = by_columns(odd[f, 0:8].reshape(CELLS, 10 * CIN), taps1[0])
        total = total + by_columns(even[f].reshape(CELLS, 10 * CIN), taps1[1])
        total = total + by_columns(odd[f, 1:9].reshape(CELLS, 10 * CIN), taps1[2])
        maps[:, f * C1 : (f + 1) * C1] = silu(total).astype(jnp.bfloat16)
    for x in range(8):
        found = by_columns(picks2[...], maps[x * 64 : (x + 1) * 64, :]).astype(jnp.bfloat16)
        for f in range(2):
            for k in range(9):
                near[f, x + 1, :, k * C1 : (k + 1) * C1] = found[
                    k * 64 : (k + 1) * 64, f * C1 : (f + 1) * C1
                ]
    for f in range(2):
        total = by_columns(near[f, 0:8].reshape(CELLS, 9 * C1), taps2[0])
        total = total + by_columns(near[f, 1:9].reshape(CELLS, 9 * C1), taps2[1])
        total = total + by_columns(near[f, 2:10].reshape(CELLS, 9 * C1), taps2[2])
        kept = jnp.where(first_frame + 2 * pair + f < length, silu(total), 0.0)
        second[2 * pair + f] = kept.astype(jnp.bfloat16)


def mixing_kernel(
    count,
    scenes,
    length_ref,
    occupancy_ref,
    conv1_ref,
    conv2_ref,
    picks1,
    picks2,
    temporal_ref,
    query_ref,
    key_ref,
    value_ref,
    out_weight_ref,
    encoded_ref,
    loss_ref,
    tall1,
    tall2,
    taps1,
    taps2,
    even,
    odd,
    maps,
    near,
    second,
    gathered,
    residual,
    q_rows,
    k_rows,
    v_rows,
    att_rows,
    done_rows,
    returned,
    total,
    frame_sums,
    scene_sums,
    there_send,
    there_recv,
    back_send,
    back_recv,
    frame_send,
    frame_recv,
    scene_send,
    scene_recv,
):
    f_dev = occupancy_ref.shape[0]
    pairs = f_dev // 2
    cells = CELLS // count
    part = cells // CHUNKS
    rows = FRAMES * part
    me = lax.axis_index("frame")
    my_scene = lax.axis_index("scene")
    length = length_ref[0]

    barrier = pltpu.get_barrier_semaphore()

    def greet_frame(d, carry):
        pl.semaphore_signal(
            barrier,
            inc=1,
            device_id={"frame": lax.rem(me + d, count)},
            device_id_type=pl.DeviceIdType.MESH,
        )
        return carry

    def greet_scene(d, carry):
        pl.semaphore_signal(
            barrier,
            inc=1,
            device_id={"scene": lax.rem(my_scene + d, scenes)},
            device_id_type=pl.DeviceIdType.MESH,
        )
        return carry

    lax.fori_loop(1, count, greet_frame, 0)
    lax.fori_loop(1, scenes, greet_scene, 0)

    def cells_of(device, chunk):
        return pl.ds(pl.multiple_of(device * cells + chunk * part, part), part)

    def there(chunk, pair, d):
        to = lax.rem(me + d, count)
        return pltpu.make_async_remote_copy(
            src_ref=second.at[pl.ds(2 * pair, 2), cells_of(to, chunk), :],
            dst_ref=gathered.at[chunk, pl.ds(1 + f_dev * me + 2 * pair, 2)],
            send_sem=there_send.at[chunk * pairs + pair, d],
            recv_sem=there_recv.at[chunk * pairs + pair, d],
            device_id={"frame": to},
            device_id_type=pl.DeviceIdType.MESH,
        )

    def back(chunk, d):
        to = lax.rem(me + d, count)
        return pltpu.make_async_remote_copy(
            src_ref=done_rows.at[chunk, pl.ds(f_dev * to, f_dev)],
            dst_ref=returned.at[:, cells_of(me, chunk), :],
            send_sem=back_send.at[chunk, d],
            recv_sem=back_recv.at[chunk, d],
            device_id={"frame": to},
            device_id_type=pl.DeviceIdType.MESH,
        )

    def frame_sum(d):
        return pltpu.make_async_remote_copy(
            src_ref=total,
            dst_ref=frame_sums.at[me],
            send_sem=frame_send.at[d],
            recv_sem=frame_recv.at[d],
            device_id={"frame": lax.rem(me + d, count)},
            device_id_type=pl.DeviceIdType.MESH,
        )

    def scene_sum(d):
        return pltpu.make_async_remote_copy(
            src_ref=total,
            dst_ref=scene_sums.at[my_scene],
            send_sem=scene_send.at[d],
            recv_sem=scene_recv.at[d],
            device_id={"scene": lax.rem(my_scene + d, scenes)},
            device_id_type=pl.DeviceIdType.MESH,
        )

    def each(first, last, act):
        def step(d, carry):
            act(d)
            return carry

        lax.fori_loop(first, last, step, 0)

    order_weights(conv1_ref, conv2_ref, tall1, tall2, taps1, taps2)
    for f in range(2):
        odd[f, 0] = jnp.zeros((64, 10 * CIN), jnp.bfloat16)
        near[f, 0] = jnp.zeros((64, 9 * C1), jnp.bfloat16)
        near[f, 9] = jnp.zeros((64, 9 * C1), jnp.bfloat16)
    for chunk in range(CHUNKS):
        gathered[chunk, 0] = jnp.zeros((part, C2), jnp.bfloat16)
        gathered[chunk, FRAMES + 1] = jnp.zeros((part, C2), jnp.bfloat16)
    for pair in range(pairs):
        convolve_pair(
            pair,
            f_dev * me,
            length,
            occupancy_ref,
            picks1,
            picks2,
            taps1,
            taps2,
            even,
            odd,
            maps,
            near,
            second,
        )
        if pair == 0:
            pl.semaphore_wait(barrier, count - 1 + scenes - 1)
        for chunk in range(CHUNKS):
            each(1, count, lambda d, chunk=chunk, pair=pair: there(chunk, pair, d).start())
    for chunk in range(CHUNKS):
        gathered[chunk, pl.ds(1 + f_dev * me, f_dev)] = second[:, cells_of(me, chunk), :]

    span = 256 // part
    block = span * part
    head_of = lax.broadcasted_iota(jnp.int32, (FRAMES, C2), 1) // HD
    ones4 = (
        lax.broadcasted_iota(jnp.int32, (C2, C2), 0) // HD
        == lax.broadcasted_iota(jnp.int32, (C2, C2), 1) // HD
    ).astype(jnp.bfloat16)
    key_mask = lax.broadcasted_iota(jnp.int32, (FRAMES, C2), 1) % FRAMES < length
    low_half = lax.broadcasted_iota(jnp.int32, (FRAMES, 128), 1) < HD
    total[...] = jnp.zeros_like(total)

    for chunk in range(CHUNKS):
        for pair in range(pairs):
            each(1, count, lambda d, chunk=chunk, pair=pair: there(chunk, pair, d).wait_recv())

        def project(b, carry, chunk=chunk):
            window = gathered[chunk, pl.ds(b * span, span + 2)].reshape((span + 2) * part, C2)
            temporal = by_rows(window[:block], temporal_ref[0])
            temporal = temporal + by_rows(window[part : part + block], temporal_ref[1])
            temporal = temporal + by_rows(window[2 * part :], temporal_ref[2])
            here = window[part : part + block].astype(jnp.float32)
            mixed = (here + silu(temporal)).astype(jnp.bfloat16)
            at = pl.ds(pl.multiple_of(b * block, block), block)
            residual[at, :] = mixed
            wide = mixed.astype(jnp.float32)
            scale = lax.rsqrt(jnp.mean(wide * wide, axis=1, keepdims=True) + NORM_EPS)
            normed = (wide * scale).astype(jnp.bfloat16)
            for weight_ref, into in ((query_ref, q_rows), (key_ref, k_rows), (value_ref, v_rows)):
                made = by_rows(normed, weight_ref[...])
                into[0, at, :] = made[:, :128]
                into[1, at, :] = made[:, 128:]
            return carry

        lax.fori_loop(0, FRAMES // span, project, 0)

        def cell_rows(ref, cell):
            at = pl.ds(cell, FRAMES, stride=part)
            return jnp.concatenate([ref[0, at, :], ref[1, at, :]], axis=1).astype(jnp.bfloat16)

        def spread(found):
            zero = jnp.zeros_like(found)
            return jnp.concatenate([jnp.where(head_of == h, found, zero) for h in range(HEADS)], 0)

        def attend(cell, carry):
            queries = cell_rows(q_rows, cell)
            keys = spread(cell_rows(k_rows, cell))
            values = spread(cell_rows(v_rows, cell))
            scores = jnp.where(key_mask, by_rows(queries, keys), -1e30)
            tops = []
            for half in range(2):
                piece = scores[:, half * 128 : half * 128 + 128]
                low = jnp.max(jnp.where(low_half, piece, -1e30), axis=1, keepdims=True)
                high = jnp.max(jnp.where(low_half, -1e30, piece), axis=1, keepdims=True)
                tops.append(jnp.where(low_half, low, high))
            top = jnp.concatenate(tops, axis=1)
            weights = jnp.exp2((scores - top) * (LOG2_E * HD**-0.5)).astype(jnp.bfloat16)
            weighted = jnp.dot(weights, values, preferred_element_type=jnp.float32)
            sums = jnp.dot(weights, ones4, preferred_element_type=jnp.float32)
            attended = weighted / sums
            at = pl.ds(cell, FRAMES, stride=part)
            att_rows[0, at, :] = attended[:, :128]
            att_rows[1, at, :] = attended[:, 128:]
            return carry

        lax.fori_loop(0, part, attend, 0)

        def finish(b, carry, chunk=chunk):
            at = pl.ds(pl.multiple_of(b * block, block), block)
            attended = jnp.concatenate([att_rows[0, at, :], att_rows[1, at, :]], axis=1)
            full = residual[at, :].astype(jnp.float32) + by_rows(
                attended.astype(jnp.bfloat16), out_weight_ref[...]
            )
            frame = b * span + lax.broadcasted_iota(jnp.int32, (block, C2), 0) // part
            kept = jnp.where(frame < length, full, 0.0).astype(jnp.bfloat16)
            done_rows[chunk, pl.ds(b * span, span)] = kept.reshape(span, part, C2)
            wide = kept.astype(jnp.float32)
            squares = jnp.sum((wide * wide).reshape(block // 8, 8, C2), axis=0)
            total[...] += squares[:, :128] + squares[:, 128:]
            return carry

        lax.fori_loop(0, FRAMES // span, finish, 0)
        each(1, count, lambda d, chunk=chunk: back(chunk, d).start())
        returned[:, cells_of(me, chunk), :] = done_rows[chunk, pl.ds(f_dev * me, f_dev)]

    each(1, count, lambda d: frame_sum(d).start())
    frame_sums[me] = total[...]
    each(1, count, lambda d: frame_sum(d).wait_recv())
    each(1, count, lambda d: frame_sum(d).wait_send())
    total[...] = jnp.sum(frame_sums[...], axis=0)
    each(1, scenes, lambda d: scene_sum(d).start())
    scene_sums[my_scene] = total[...]

    eye = (
        lax.broadcasted_iota(jnp.int32, (C2, C2), 0)
        == lax.broadcasted_iota(jnp.int32, (C2, C2), 1)
    ).astype(jnp.bfloat16)
    for chunk in range(CHUNKS):
        each(1, count, lambda d, chunk=chunk: back(chunk, d).wait_recv())

    def turn(f, carry):
        encoded_ref[f] = by_rows(eye, returned[f]).astype(jnp.bfloat16)
        return carry

    lax.fori_loop(0, f_dev, turn, 0)

    each(1, scenes, lambda d: scene_sum(d).wait_recv())
    loss_ref[...] = jnp.sum(scene_sums[...], axis=0)
    each(1, scenes, lambda d: scene_sum(d).wait_send())
    for chunk in range(CHUNKS):
        for pair in range(pairs):
            each(1, count, lambda d, chunk=chunk, pair=pair: there(chunk, pair, d).wait_send())
        each(1, count, lambda d, chunk=chunk: back(chunk, d).wait_send())


def shards(
    occupancy,
    scene_lengths,
    conv1_weight,
    conv2_weight,
    temporal_weight,
    query_weight,
    key_weight,
    value_weight,
    out_weight,
):
    f_dev = occupancy.shape[1]
    count, scenes = lax.axis_size("frame"), lax.axis_size("scene")
    part = CELLS // count // CHUNKS
    rows = FRAMES * part
    wide_rows = pltpu.VMEM((2, rows, 128), jnp.float32)
    in_vmem = pl.BlockSpec(memory_space=pltpu.VMEM)
    encoded, sums = pl.pallas_call(
        functools.partial(mixing_kernel, count, scenes),
        out_shape=(
            jax.ShapeDtypeStruct((f_dev, C2, CELLS), jnp.bfloat16),
            jax.ShapeDtypeStruct((8, 128), jnp.float32),
        ),
        in_specs=[pl.BlockSpec(memory_space=pltpu.SMEM)] + [in_vmem] * 10,
        out_specs=(in_vmem, in_vmem),
        scratch_shapes=[
            pltpu.VMEM((CIN * 27, C1), jnp.float32),
            pltpu.VMEM((2, C1 * 27, 128), jnp.float32),
            pltpu.VMEM((3, 10 * CIN, C1), jnp.bfloat16),
            pltpu.VMEM((3, 9 * C1, C2), jnp.bfloat16),
            pltpu.VMEM((2, 8, 64, 10 * CIN), jnp.bfloat16),
            pltpu.VMEM((2, 9, 64, 10 * CIN), jnp.bfloat16),
            pltpu.VMEM((CELLS, 2 * C1), jnp.bfloat16),
            pltpu.VMEM((2, 10, 64, 9 * C1), jnp.bfloat16),
            pltpu.VMEM((f_dev, CELLS, C2), jnp.bfloat16),
            pltpu.VMEM((CHUNKS, FRAMES + 2, part, C2), jnp.bfloat16),
            pltpu.VMEM((rows, C2), jnp.bfloat16),
            wide_rows,
            wide_rows,
            wide_rows,
            wide_rows,
            pltpu.VMEM((CHUNKS, FRAMES, part, C2), jnp.bfloat16),
            pltpu.VMEM((f_dev, CELLS, C2), jnp.bfloat16),
            pltpu.VMEM((8, 128), jnp.float32),
            pltpu.VMEM((count, 8, 128), jnp.float32),
            pltpu.VMEM((scenes, 8, 128), jnp.float32),
        ]
        + [pltpu.SemaphoreType.DMA((CHUNKS * f_dev // 2, count))] * 2
        + [pltpu.SemaphoreType.DMA((CHUNKS, count))] * 2
        + [pltpu.SemaphoreType.DMA((count,))] * 2
        + [pltpu.SemaphoreType.DMA((scenes,))] * 2,
        compiler_params=pltpu.CompilerParams(
            collective_id=0, has_side_effects=True, vmem_limit_bytes=48 * 2**20
        ),
    )(
        scene_lengths,
        occupancy[0],
        conv1_weight.T,
        conv2_weight,
        jnp.asarray(picks_strided(), jnp.bfloat16),
        jnp.asarray(picks_near(), jnp.bfloat16),
        temporal_weight,
        query_weight,
        key_weight,
        value_weight,
        out_weight,
    )
    slot_count = float(scenes * FRAMES * CELLS * C2)
    kl_loss = 0.5 * jnp.sum(sums) / slot_count
    return (encoded[None], kl_loss)


def solution(mesh):
    placed = (P("scene", "frame", None, None), P("scene"), P(), P(), P(), P(), P(), P(), P())
    return jax.shard_map(
        shards,
        mesh=mesh,
        in_specs=placed,
        out_specs=(P("scene", "frame", None, None), P()),
        check_vma=False,
    )
```

```python
import functools

import jax
import jax.numpy as jnp
import numpy as np
from jax import lax
from jax.experimental import pallas as pl
from jax.experimental.pallas import tpu as pltpu
from jax.sharding import PartitionSpec as P

CIN = 64
C1 = 128
C2 = 256
HEADS = 4
HD = 64
HI = 16
ZD = 8
CELLS = 512


NORM_EPS = 1e-06


FRAMES = 64
CHUNKS = 2
LOG2_E = 1.4426950408889634


def by_rows(rows, weight):
    return lax.dot_general(
        rows, weight, (((1,), (1,)), ((), ())), preferred_element_type=jnp.float32
    )


def by_columns(rows, matrix):
    return jnp.dot(rows, matrix, preferred_element_type=jnp.float32)


def silu(v):
    return 0.5 * v * (1.0 + jnp.tanh(0.5 * v))


def picks_strided():
    picks = np.zeros((5, 8, ZD, 2, HI, ZD), np.float32)
    for tap in range(9):
        for out_y in range(8):
            for out_z in range(ZD):
                y, z = 2 * out_y + tap // 3 - 1, out_z + tap % 3 - 1
                if 0 <= y < HI and 0 <= z < ZD:
                    picks[tap // 2, out_y, out_z, tap % 2, y, z] = 1
    return picks.reshape(5 * 64, 2 * HI * ZD)


def picks_near():
    picks = np.zeros((9, 8, ZD, 8, ZD), np.float32)
    for tap in range(9):
        for out_y in range(8):
            for out_z in range(ZD):
                y, z = out_y + tap // 3 - 1, out_z + tap % 3 - 1
                if 0 <= y < 8 and 0 <= z < ZD:
                    picks[tap, out_y, out_z, y, z] = 1
    return picks.reshape(9 * 64, 64)


def order_weights(conv1_ref, conv2_ref, tall1, tall2, taps1, taps2):
    eye = (
        lax.broadcasted_iota(jnp.int32, (128, 128), 0)
        == lax.broadcasted_iota(jnp.int32, (128, 128), 1)
    ).astype(jnp.bfloat16)
    tall1[...] = conv1_ref[...].astype(jnp.float32)
    for at in range(0, C1 * 27, 128):
        turned = by_rows(eye, conv2_ref[:, at : at + 128])
        tall2[0, at : at + 128, :] = turned[:, :128]
        tall2[1, at : at + 128, :] = turned[:, 128:]
    for dx in range(3):
        for tap in range(9):
            at = pl.ds(dx * 9 + tap, CIN, stride=27)
            taps1[dx, tap * CIN : (tap + 1) * CIN, :] = tall1[at, :].astype(jnp.bfloat16)
            at = pl.ds(dx * 9 + tap, C1, stride=27)
            taps2[dx, tap * C1 : (tap + 1) * C1, :] = jnp.concatenate(
                [tall2[0, at, :], tall2[1, at, :]], axis=1
            ).astype(jnp.bfloat16)
        taps1[dx, 9 * CIN :, :] = jnp.zeros((CIN, C1), jnp.bfloat16)


def convolve_pair(
    pair, first_frame, length, occupancy_ref, picks1, picks2, taps1, taps2, even, odd, maps, near, second
):
    blank = jnp.zeros((CIN, 128), jnp.bfloat16)
    for x in range(HI):
        pieces = []
        for f in range(2):
            plane = occupancy_ref[2 * pair + f, :, x * 128 : (x + 1) * 128]
            pieces.append(jnp.concatenate([plane, blank], axis=1))
            pieces.append(jnp.concatenate([blank, plane], axis=1))
        found = by_rows(picks1[...], jnp.concatenate(pieces, axis=0)).astype(jnp.bfloat16)
        into, row = (even, x // 2) if x % 2 == 0 else (odd, x // 2 + 1)
        for f in range(2):
            for k in range(5):
                into[f, row, :, k * 128 : (k + 1) * 128] = found[
                    k * 64 : (k + 1) * 64, f * 128 : (f + 1) * 128
                ]
    for f in range(2):
        total = by_columns(odd[f, 0:8].reshape(CELLS, 10 * CIN), taps1[0])
        total = total + by_columns(even[f].reshape(CELLS, 10 * CIN), taps1[1])
        total = total + by_columns(odd[f, 1:9].reshape(CELLS, 10 * CIN), taps1[2])
        maps[:, f * C1 : (f + 1) * C1] = silu(total).astype(jnp.bfloat16)
    for x in range(8):
        found = by_columns(picks2[...], maps[x * 64 : (x + 1) * 64, :]).astype(jnp.bfloat16)
        for f in range(2):
            for k in range(9):
                near[f, x + 1, :, k * C1 : (k + 1) * C1] = found[
                    k * 64 : (k + 1) * 64, f * C1 : (f + 1) * C1
                ]
    for f in range(2):
        total = by_columns(near[f, 0:8].reshape(CELLS, 9 * C1), taps2[0])
        total = total + by_columns(near[f, 1:9].reshape(CELLS, 9 * C1), taps2[1])
        total = total + by_columns(near[f, 2:10].reshape(CELLS, 9 * C1), taps2[2])
        kept = jnp.where(first_frame + 2 * pair + f < length, silu(total), 0.0)
        second[2 * pair + f] = kept.astype(jnp.bfloat16)


def mixing_kernel(
    count,
    scenes,
    length_ref,
    occupancy_in,
    picks1_in,
    conv1_in,
    conv2_in,
    picks2_in,
    temporal_in,
    query_in,
    key_in,
    value_in,
    out_weight_in,
    encoded_ref,
    loss_ref,
    occupancy_ref,
    picks1,
    conv1_ref,
    conv2_ref,
    picks2,
    temporal_ref,
    query_ref,
    key_ref,
    value_ref,
    out_weight_ref,
    tall1,
    tall2,
    taps1,
    taps2,
    even,
    odd,
    maps,
    near,
    second,
    gathered,
    residual,
    q_rows,
    k_rows,
    v_rows,
    att_rows,
    done_rows,
    returned,
    total,
    frame_sums,
    scene_sums,
    there_send,
    there_recv,
    back_send,
    back_recv,
    frame_send,
    frame_recv,
    scene_send,
    scene_recv,
    load_sem,
):
    f_dev = occupancy_ref.shape[0]
    pairs = f_dev // 2
    cells = CELLS // count
    part = cells // CHUNKS
    rows = FRAMES * part
    me = lax.axis_index("frame")
    my_scene = lax.axis_index("scene")
    length = length_ref[0]

    loads = [
        pltpu.make_async_copy(source, into, load_sem.at[i])
        for i, (source, into) in enumerate(
            (
                (occupancy_in, occupancy_ref),
                (picks1_in, picks1),
                (conv1_in, conv1_ref),
                (conv2_in, conv2_ref),
                (picks2_in, picks2),
                (temporal_in, temporal_ref),
                (query_in, query_ref),
                (key_in, key_ref),
                (value_in, value_ref),
                (out_weight_in, out_weight_ref),
            )
        )
    ]
    for load in loads:
        load.start()

    barrier = pltpu.get_barrier_semaphore()

    def greet_frame(d, carry):
        pl.semaphore_signal(
            barrier,
            inc=1,
            device_id={"frame": lax.rem(me + d, count)},
            device_id_type=pl.DeviceIdType.MESH,
        )
        return carry

    def greet_scene(d, carry):
        pl.semaphore_signal(
            barrier,
            inc=1,
            device_id={"scene": lax.rem(my_scene + d, scenes)},
            device_id_type=pl.DeviceIdType.MESH,
        )
        return carry

    lax.fori_loop(1, count, greet_frame, 0)
    lax.fori_loop(1, scenes, greet_scene, 0)

    def cells_of(device, chunk):
        return pl.ds(pl.multiple_of(device * cells + chunk * part, part), part)

    def there(chunk, pair, d):
        to = lax.rem(me + d, count)
        return pltpu.make_async_remote_copy(
            src_ref=second.at[pl.ds(2 * pair, 2), cells_of(to, chunk), :],
            dst_ref=gathered.at[chunk, pl.ds(1 + f_dev * me + 2 * pair, 2)],
            send_sem=there_send.at[chunk * pairs + pair, d],
            recv_sem=there_recv.at[chunk * pairs + pair, d],
            device_id={"frame": to},
            device_id_type=pl.DeviceIdType.MESH,
        )

    def back(chunk, d):
        to = lax.rem(me + d, count)
        return pltpu.make_async_remote_copy(
            src_ref=done_rows.at[chunk, pl.ds(f_dev * to, f_dev)],
            dst_ref=returned.at[:, cells_of(me, chunk), :],
            send_sem=back_send.at[chunk, d],
            recv_sem=back_recv.at[chunk, d],
            device_id={"frame": to},
            device_id_type=pl.DeviceIdType.MESH,
        )

    def frame_sum(d):
        return pltpu.make_async_remote_copy(
            src_ref=total,
            dst_ref=frame_sums.at[me],
            send_sem=frame_send.at[d],
            recv_sem=frame_recv.at[d],
            device_id={"frame": lax.rem(me + d, count)},
            device_id_type=pl.DeviceIdType.MESH,
        )

    def scene_sum(d):
        return pltpu.make_async_remote_copy(
            src_ref=total,
            dst_ref=scene_sums.at[my_scene],
            send_sem=scene_send.at[d],
            recv_sem=scene_recv.at[d],
            device_id={"scene": lax.rem(my_scene + d, scenes)},
            device_id_type=pl.DeviceIdType.MESH,
        )

    def each(first, last, act):
        def step(d, carry):
            act(d)
            return carry

        lax.fori_loop(first, last, step, 0)

    for load in loads[:5]:
        load.wait()
    order_weights(conv1_ref, conv2_ref, tall1, tall2, taps1, taps2)
    for f in range(2):
        odd[f, 0] = jnp.zeros((64, 10 * CIN), jnp.bfloat16)
        near[f, 0] = jnp.zeros((64, 9 * C1), jnp.bfloat16)
        near[f, 9] = jnp.zeros((64, 9 * C1), jnp.bfloat16)
    for chunk in range(CHUNKS):
        gathered[chunk, 0] = jnp.zeros((part, C2), jnp.bfloat16)
        gathered[chunk, FRAMES + 1] = jnp.zeros((part, C2), jnp.bfloat16)
    for pair in range(pairs):
        convolve_pair(
            pair,
            f_dev * me,
            length,
            occupancy_ref,
            picks1,
            picks2,
            taps1,
            taps2,
            even,
            odd,
            maps,
            near,
            second,
        )
        if pair == 0:
            pl.semaphore_wait(barrier, count - 1 + scenes - 1)
        for chunk in range(CHUNKS):
            each(1, count, lambda d, chunk=chunk, pair=pair: there(chunk, pair, d).start())
    for chunk in range(CHUNKS):
        gathered[chunk, pl.ds(1 + f_dev * me, f_dev)] = second[:, cells_of(me, chunk), :]

    for load in loads[5:]:
        load.wait()

    span = 256 // part
    block = span * part
    head_of = lax.broadcasted_iota(jnp.int32, (FRAMES, C2), 1) // HD
    ones4 = (
        lax.broadcasted_iota(jnp.int32, (C2, C2), 0) // HD
        == lax.broadcasted_iota(jnp.int32, (C2, C2), 1) // HD
    ).astype(jnp.bfloat16)
    key_mask = lax.broadcasted_iota(jnp.int32, (FRAMES, C2), 1) % FRAMES < length
    low_half = lax.broadcasted_iota(jnp.int32, (FRAMES, 128), 1) < HD
    total[...] = jnp.zeros_like(total)

    for chunk in range(CHUNKS):
        for pair in range(pairs):
            each(1, count, lambda d, chunk=chunk, pair=pair: there(chunk, pair, d).wait_recv())

        def project(b, carry, chunk=chunk):
            window = gathered[chunk, pl.ds(b * span, span + 2)].reshape((span + 2) * part, C2)
            temporal = by_rows(window[:block], temporal_ref[0])
            temporal = temporal + by_rows(window[part : part + block], temporal_ref[1])
            temporal = temporal + by_rows(window[2 * part :], temporal_ref[2])
            here = window[part : part + block].astype(jnp.float32)
            mixed = (here + silu(temporal)).astype(jnp.bfloat16)
            at = pl.ds(pl.multiple_of(b * block, block), block)
            residual[at, :] = mixed
            wide = mixed.astype(jnp.float32)
            scale = lax.rsqrt(jnp.mean(wide * wide, axis=1, keepdims=True) + NORM_EPS)
            normed = (wide * scale).astype(jnp.bfloat16)
            for weight_ref, into in ((query_ref, q_rows), (key_ref, k_rows), (value_ref, v_rows)):
                made = by_rows(normed, weight_ref[...])
                into[0, at, :] = made[:, :128]
                into[1, at, :] = made[:, 128:]
            return carry

        lax.fori_loop(0, FRAMES // span, project, 0, unroll=True)

        def cell_rows(ref, cell):
            at = pl.ds(cell, FRAMES, stride=part)
            return jnp.concatenate([ref[0, at, :], ref[1, at, :]], axis=1).astype(jnp.bfloat16)

        def spread(found):
            zero = jnp.zeros_like(found)
            return jnp.concatenate([jnp.where(head_of == h, found, zero) for h in range(HEADS)], 0)

        def attend(cell, carry):
            queries = cell_rows(q_rows, cell)
            keys = spread(cell_rows(k_rows, cell))
            values = spread(cell_rows(v_rows, cell))
            scores = jnp.where(key_mask, by_rows(queries, keys), -1e30)
            tops = []
            for half in range(2):
                piece = scores[:, half * 128 : half * 128 + 128]
                low = jnp.max(jnp.where(low_half, piece, -1e30), axis=1, keepdims=True)
                high = jnp.max(jnp.where(low_half, -1e30, piece), axis=1, keepdims=True)
                tops.append(jnp.where(low_half, low, high))
            top = jnp.concatenate(tops, axis=1)
            weights = jnp.exp2((scores - top) * (LOG2_E * HD**-0.5)).astype(jnp.bfloat16)
            weighted = jnp.dot(weights, values, preferred_element_type=jnp.float32)
            sums = jnp.dot(weights, ones4, preferred_element_type=jnp.float32)
            attended = weighted / sums
            at = pl.ds(cell, FRAMES, stride=part)
            att_rows[0, at, :] = attended[:, :128]
            att_rows[1, at, :] = attended[:, 128:]
            return carry

        lax.fori_loop(0, part, attend, 0, unroll=True)

        def finish(b, carry, chunk=chunk):
            at = pl.ds(pl.multiple_of(b * block, block), block)
            attended = jnp.concatenate([att_rows[0, at, :], att_rows[1, at, :]], axis=1)
            full = residual[at, :].astype(jnp.float32) + by_rows(
                attended.astype(jnp.bfloat16), out_weight_ref[...]
            )
            frame = b * span + lax.broadcasted_iota(jnp.int32, (block, C2), 0) // part
            kept = jnp.where(frame < length, full, 0.0).astype(jnp.bfloat16)
            done_rows[chunk, pl.ds(b * span, span)] = kept.reshape(span, part, C2)
            wide = kept.astype(jnp.float32)
            squares = jnp.sum((wide * wide).reshape(block // 8, 8, C2), axis=0)
            total[...] += squares[:, :128] + squares[:, 128:]
            return carry

        lax.fori_loop(0, FRAMES // span, finish, 0, unroll=True)
        each(1, count, lambda d, chunk=chunk: back(chunk, d).start())
        returned[:, cells_of(me, chunk), :] = done_rows[chunk, pl.ds(f_dev * me, f_dev)]

    each(1, count, lambda d: frame_sum(d).start())
    frame_sums[me] = total[...]
    each(1, count, lambda d: frame_sum(d).wait_recv())
    each(1, count, lambda d: frame_sum(d).wait_send())
    total[...] = jnp.sum(frame_sums[...], axis=0)
    each(1, scenes, lambda d: scene_sum(d).start())
    scene_sums[my_scene] = total[...]

    for chunk in range(CHUNKS):
        each(1, count, lambda d, chunk=chunk: back(chunk, d).wait_recv())

    for f in range(f_dev):
        encoded_ref[f] = returned[f].T

    each(1, scenes, lambda d: scene_sum(d).wait_recv())
    loss_ref[...] = jnp.sum(scene_sums[...], axis=0)
    each(1, scenes, lambda d: scene_sum(d).wait_send())
    for chunk in range(CHUNKS):
        for pair in range(pairs):
            each(1, count, lambda d, chunk=chunk, pair=pair: there(chunk, pair, d).wait_send())
        each(1, count, lambda d, chunk=chunk: back(chunk, d).wait_send())


def shards(
    occupancy,
    scene_lengths,
    conv1_weight,
    conv2_weight,
    temporal_weight,
    query_weight,
    key_weight,
    value_weight,
    out_weight,
):
    f_dev = occupancy.shape[1]
    count, scenes = lax.axis_size("frame"), lax.axis_size("scene")
    operands = (
        occupancy[0],
        jnp.asarray(picks_strided(), jnp.bfloat16),
        conv1_weight.T,
        conv2_weight,
        jnp.asarray(picks_near(), jnp.bfloat16),
        temporal_weight,
        query_weight,
        key_weight,
        value_weight,
        out_weight,
    )
    part = CELLS // count // CHUNKS
    rows = FRAMES * part
    wide_rows = pltpu.VMEM((2, rows, 128), jnp.float32)
    in_vmem = pl.BlockSpec(memory_space=pltpu.VMEM)
    encoded, sums = pl.pallas_call(
        functools.partial(mixing_kernel, count, scenes),
        out_shape=(
            jax.ShapeDtypeStruct((f_dev, C2, CELLS), jnp.bfloat16),
            jax.ShapeDtypeStruct((8, 128), jnp.float32),
        ),
        in_specs=[pl.BlockSpec(memory_space=pltpu.SMEM)] + [pl.BlockSpec(memory_space=pl.ANY)] * 10,
        out_specs=(in_vmem, in_vmem),
        scratch_shapes=[pltpu.VMEM(array.shape, array.dtype) for array in operands]
        + [
            pltpu.VMEM((CIN * 27, C1), jnp.float32),
            pltpu.VMEM((2, C1 * 27, 128), jnp.float32),
            pltpu.VMEM((3, 10 * CIN, C1), jnp.bfloat16),
            pltpu.VMEM((3, 9 * C1, C2), jnp.bfloat16),
            pltpu.VMEM((2, 8, 64, 10 * CIN), jnp.bfloat16),
            pltpu.VMEM((2, 9, 64, 10 * CIN), jnp.bfloat16),
            pltpu.VMEM((CELLS, 2 * C1), jnp.bfloat16),
            pltpu.VMEM((2, 10, 64, 9 * C1), jnp.bfloat16),
            pltpu.VMEM((f_dev, CELLS, C2), jnp.bfloat16),
            pltpu.VMEM((CHUNKS, FRAMES + 2, part, C2), jnp.bfloat16),
            pltpu.VMEM((rows, C2), jnp.bfloat16),
            wide_rows,
            wide_rows,
            wide_rows,
            wide_rows,
            pltpu.VMEM((CHUNKS, FRAMES, part, C2), jnp.bfloat16),
            pltpu.VMEM((f_dev, CELLS, C2), jnp.bfloat16),
            pltpu.VMEM((8, 128), jnp.float32),
            pltpu.VMEM((count, 8, 128), jnp.float32),
            pltpu.VMEM((scenes, 8, 128), jnp.float32),
        ]
        + [pltpu.SemaphoreType.DMA((CHUNKS * f_dev // 2, count))] * 2
        + [pltpu.SemaphoreType.DMA((CHUNKS, count))] * 2
        + [pltpu.SemaphoreType.DMA((count,))] * 2
        + [pltpu.SemaphoreType.DMA((scenes,))] * 2
        + [pltpu.SemaphoreType.DMA((10,))],
        compiler_params=pltpu.CompilerParams(
            collective_id=0, has_side_effects=True, vmem_limit_bytes=60 * 2**20
        ),
    )(scene_lengths, *operands)
    slot_count = float(scenes * FRAMES * CELLS * C2)
    kl_loss = 0.5 * jnp.sum(sums) / slot_count
    return (encoded[None], kl_loss)


def solution(mesh):
    placed = (P("scene", "frame", None, None), P("scene"), P(), P(), P(), P(), P(), P(), P())
    return jax.shard_map(
        shards,
        mesh=mesh,
        in_specs=placed,
        out_specs=(P("scene", "frame", None, None), P()),
        check_vma=False,
    )
```

```python
import functools

import jax
import jax.numpy as jnp
import numpy as np
from jax import lax
from jax.experimental import pallas as pl
from jax.experimental.pallas import tpu as pltpu
from jax.sharding import PartitionSpec as P

CIN = 64
C1 = 128
C2 = 256
HEADS = 4
HD = 64
HI = 16
ZD = 8
CELLS = 512


NORM_EPS = 1e-06


FRAMES = 64
CHUNKS = 2
SIDE = 4
HALF_WAY = 8
OFFSETS = (
    (2, 2),
    (2, 1),
    (2, 3),
    (1, 2),
    (3, 2),
    (2, 0),
    (0, 2),
    (1, 1),
    (3, 3),
    (1, 3),
    (3, 1),
    (0, 1),
    (0, 3),
    (1, 0),
    (3, 0),
)
LOG2_E = 1.4426950408889634


def by_rows(rows, weight):
    return lax.dot_general(
        rows, weight, (((1,), (1,)), ((), ())), preferred_element_type=jnp.float32
    )


def by_columns(rows, matrix):
    return jnp.dot(rows, matrix, preferred_element_type=jnp.float32)


def silu(v):
    return 0.5 * v * (1.0 + jnp.tanh(0.5 * v))


def picks_strided():
    picks = np.zeros((5, 8, ZD, 2, HI, ZD), np.float32)
    for tap in range(9):
        for out_y in range(8):
            for out_z in range(ZD):
                y, z = 2 * out_y + tap // 3 - 1, out_z + tap % 3 - 1
                if 0 <= y < HI and 0 <= z < ZD:
                    picks[tap // 2, out_y, out_z, tap % 2, y, z] = 1
    return picks.reshape(5 * 64, 2 * HI * ZD)


def picks_near():
    picks = np.zeros((9, 8, ZD, 8, ZD), np.float32)
    for tap in range(9):
        for out_y in range(8):
            for out_z in range(ZD):
                y, z = out_y + tap // 3 - 1, out_z + tap % 3 - 1
                if 0 <= y < 8 and 0 <= z < ZD:
                    picks[tap, out_y, out_z, y, z] = 1
    return picks.reshape(9 * 64, 64)


def order_first(conv1_ref, tall1, taps1):
    tall1[...] = conv1_ref[...].astype(jnp.float32)
    for dx in range(3):
        for tap in range(9):
            at = pl.ds(dx * 9 + tap, CIN, stride=27)
            taps1[dx, tap * CIN : (tap + 1) * CIN, :] = tall1[at, :].astype(jnp.bfloat16)
        taps1[dx, 9 * CIN :, :] = jnp.zeros((CIN, C1), jnp.bfloat16)


def order_second(conv2_ref, tall2, taps2):
    eye = (
        lax.broadcasted_iota(jnp.int32, (128, 128), 0)
        == lax.broadcasted_iota(jnp.int32, (128, 128), 1)
    ).astype(jnp.bfloat16)
    for at in range(0, C1 * 27, 128):
        turned = by_rows(eye, conv2_ref[:, at : at + 128])
        tall2[0, at : at + 128, :] = turned[:, :128]
        tall2[1, at : at + 128, :] = turned[:, 128:]
    for dx in range(3):
        for tap in range(9):
            at = pl.ds(dx * 9 + tap, C1, stride=27)
            taps2[dx, tap * C1 : (tap + 1) * C1, :] = jnp.concatenate(
                [tall2[0, at, :], tall2[1, at, :]], axis=1
            ).astype(jnp.bfloat16)


def convolve_pair(
    pair, first_frame, length, ready, send, occupancy_ref, picks1, picks2, taps1, taps2, even, odd, maps, near, second
):
    blank = jnp.zeros((CIN, 128), jnp.bfloat16)
    for x in range(HI):
        pieces = []
        for f in range(2):
            plane = occupancy_ref[2 * pair + f, :, x * 128 : (x + 1) * 128]
            pieces.append(jnp.concatenate([plane, blank], axis=1))
            pieces.append(jnp.concatenate([blank, plane], axis=1))
        found = by_rows(picks1[...], jnp.concatenate(pieces, axis=0)).astype(jnp.bfloat16)
        into, row = (even, x // 2) if x % 2 == 0 else (odd, x // 2 + 1)
        for f in range(2):
            for k in range(5):
                into[f, row, :, k * 128 : (k + 1) * 128] = found[
                    k * 64 : (k + 1) * 64, f * 128 : (f + 1) * 128
                ]
    ready(1)
    for f in range(2):
        planes = [odd[f, 0:8], even[f], odd[f, 1:9]]
        planes = jnp.concatenate([p.reshape(CELLS, 10 * CIN) for p in planes], axis=1)
        total = by_columns(planes, taps1[...].reshape(30 * CIN, C1))
        maps[:, f * C1 : (f + 1) * C1] = silu(total).astype(jnp.bfloat16)
    ready(2)
    for x in range(8):
        found = by_columns(picks2[...], maps[x * 64 : (x + 1) * 64, :]).astype(jnp.bfloat16)
        for f in range(2):
            for k in range(9):
                near[f, x + 1, :, k * C1 : (k + 1) * C1] = found[
                    k * 64 : (k + 1) * 64, f * C1 : (f + 1) * C1
                ]
    for f in range(2):
        planes = [near[f, dx : dx + 8].reshape(CELLS, 9 * C1) for dx in range(3)]
        total = by_columns(jnp.concatenate(planes, axis=1), taps2[...].reshape(27 * C1, C2))
        kept = jnp.where(first_frame + 2 * pair + f < length, silu(total), 0.0)
        second[2 * pair + f] = kept.astype(jnp.bfloat16)
        send(2 * pair + f)


def mixing_kernel(
    count,
    scenes,
    length_ref,
    occupancy_in,
    picks1_in,
    conv1_in,
    conv2_in,
    picks2_in,
    temporal_in,
    query_in,
    key_in,
    value_in,
    out_weight_in,
    encoded_ref,
    loss_ref,
    occupancy_ref,
    picks1,
    conv1_ref,
    conv2_ref,
    picks2,
    temporal_ref,
    query_ref,
    key_ref,
    value_ref,
    out_weight_ref,
    tall1,
    tall2,
    taps1,
    taps2,
    even,
    odd,
    maps,
    near,
    second,
    gathered,
    residual,
    q_rows,
    k_rows,
    v_rows,
    att_rows,
    done_rows,
    returned,
    total,
    group_total,
    frame_sums,
    scene_sums,
    there_send,
    there_recv,
    back_send,
    back_recv,
    frame_send,
    frame_recv,
    scene_send,
    scene_recv,
    load_sem,
):
    f_dev = occupancy_ref.shape[0]
    pairs = f_dev // 2
    cells = CELLS // count
    part = cells // CHUNKS
    rows = FRAMES * part
    me = lax.axis_index("frame")
    my_scene = lax.axis_index("scene")
    length = length_ref[0]

    loads = [
        pltpu.make_async_copy(source, into, load_sem.at[i])
        for i, (source, into) in enumerate(
            (
                (occupancy_in, occupancy_ref),
                (picks1_in, picks1),
                (conv1_in, conv1_ref),
                (conv2_in, conv2_ref),
                (picks2_in, picks2),
                (temporal_in, temporal_ref),
                (query_in, query_ref),
                (key_in, key_ref),
                (value_in, value_ref),
                (out_weight_in, out_weight_ref),
            )
        )
    ]
    for load in loads:
        load.start()

    barrier = pltpu.get_barrier_semaphore()

    def greet_frame(d, carry):
        pl.semaphore_signal(
            barrier,
            inc=1,
            device_id={"frame": lax.rem(me + d, count)},
            device_id_type=pl.DeviceIdType.MESH,
        )
        return carry

    def greet_scene(d, carry):
        pl.semaphore_signal(
            barrier,
            inc=1,
            device_id={"scene": lax.rem(my_scene + d, scenes)},
            device_id_type=pl.DeviceIdType.MESH,
        )
        return carry

    lax.fori_loop(1, count, greet_frame, 0)
    lax.fori_loop(1, scenes, greet_scene, 0)

    def cells_of(device, chunk):
        return pl.ds(pl.multiple_of(device * cells + chunk * part, part), part)

    pieces = [(frame, 1, 0, cells) for frame in range(f_dev - 2)]
    pieces += [(f_dev - 2, 2, chunk * part, part) for chunk in range(CHUNKS)]

    def peer(d):
        down, across = OFFSETS[d - 1]
        return lax.rem(me // SIDE + down, SIDE) * SIDE + lax.rem(me + across, SIDE)

    def there(piece, d):
        frame, frames, first, size = pieces[piece]
        to = peer(d)
        return pltpu.make_async_remote_copy(
            src_ref=second.at[
                pl.ds(frame, frames), pl.ds(pl.multiple_of(to * cells + first, part), size), :
            ],
            dst_ref=gathered.at[pl.ds(1 + f_dev * me + frame, frames), pl.ds(first, size)],
            send_sem=there_send.at[piece, d],
            recv_sem=there_recv.at[piece, d],
            device_id={"frame": to},
            device_id_type=pl.DeviceIdType.MESH,
        )

    def back(chunk, d):
        to = peer(d)
        return pltpu.make_async_remote_copy(
            src_ref=done_rows.at[chunk, pl.ds(f_dev * to, f_dev)],
            dst_ref=returned.at[:, cells_of(me, chunk), :],
            send_sem=back_send.at[chunk, d],
            recv_sem=back_recv.at[chunk, d],
            device_id={"frame": to},
            device_id_type=pl.DeviceIdType.MESH,
        )

    def frame_sum(d):
        return pltpu.make_async_remote_copy(
            src_ref=total,
            dst_ref=frame_sums.at[me],
            send_sem=frame_send.at[d],
            recv_sem=frame_recv.at[d],
            device_id={"frame": peer(d)},
            device_id_type=pl.DeviceIdType.MESH,
        )

    def scene_sum(d):
        return pltpu.make_async_remote_copy(
            src_ref=group_total,
            dst_ref=scene_sums.at[my_scene],
            send_sem=scene_send.at[d],
            recv_sem=scene_recv.at[d],
            device_id={"scene": lax.rem(my_scene + d, scenes)},
            device_id_type=pl.DeviceIdType.MESH,
        )

    def each(first, last, act):
        for d in range(first, last):
            act(d)

    for load in loads[:2]:
        load.wait()

    def ready(stage):
        if stage == 1:
            loads[2].wait()
            order_first(conv1_ref, tall1, taps1)
        else:
            loads[3].wait()
            loads[4].wait()
            order_second(conv2_ref, tall2, taps2)

    def send(frame):
        if frame == 0:
            pl.semaphore_wait(barrier, count - 1 + scenes - 1)
        for piece in range(len(pieces)):
            if pieces[piece][0] + pieces[piece][1] == frame + 1:
                each(1, count, lambda d, piece=piece: there(piece, d).start())

    for f in range(2):
        odd[f, 0] = jnp.zeros((64, 10 * CIN), jnp.bfloat16)
        near[f, 0] = jnp.zeros((64, 9 * C1), jnp.bfloat16)
        near[f, 9] = jnp.zeros((64, 9 * C1), jnp.bfloat16)
    gathered[0] = jnp.zeros((cells, C2), jnp.bfloat16)
    gathered[FRAMES + 1] = jnp.zeros((cells, C2), jnp.bfloat16)
    for pair in range(pairs):
        convolve_pair(
            pair,
            f_dev * me,
            length,
            ready if pair == 0 else lambda stage: None,
            send,
            occupancy_ref,
            picks1,
            picks2,
            taps1,
            taps2,
            even,
            odd,
            maps,
            near,
            second,
        )
    gathered[pl.ds(1 + f_dev * me, f_dev)] = second[
        :, pl.ds(pl.multiple_of(me * cells, cells), cells), :
    ]

    for load in loads[5:]:
        load.wait()

    span = 256 // part
    block = span * part
    head_of = lax.broadcasted_iota(jnp.int32, (FRAMES, C2), 1) // HD
    ones4 = (
        lax.broadcasted_iota(jnp.int32, (C2, C2), 0) // HD
        == lax.broadcasted_iota(jnp.int32, (C2, C2), 1) // HD
    ).astype(jnp.bfloat16)
    key_mask = lax.broadcasted_iota(jnp.int32, (FRAMES, C2), 1) % FRAMES < length
    low_half = lax.broadcasted_iota(jnp.int32, (FRAMES, 128), 1) < HD
    total[...] = jnp.zeros_like(total)

    for chunk in range(CHUNKS):
        for piece in range(len(pieces)):
            if pieces[piece][2] == chunk * part:
                each(1, count, lambda d, piece=piece: there(piece, d).wait_recv())

        def project(b, carry, chunk=chunk):
            window = gathered[pl.ds(b * span, span + 2), chunk * part : (chunk + 1) * part]
            window = window.reshape((span + 2) * part, C2)
            temporal = by_rows(window[:block], temporal_ref[0])
            temporal = temporal + by_rows(window[part : part + block], temporal_ref[1])
            temporal = temporal + by_rows(window[2 * part :], temporal_ref[2])
            here = window[part : part + block].astype(jnp.float32)
            mixed = (here + silu(temporal)).astype(jnp.bfloat16)
            at = pl.ds(pl.multiple_of(b * block, block), block)
            residual[at, :] = mixed
            wide = mixed.astype(jnp.float32)
            scale = lax.rsqrt(jnp.mean(wide * wide, axis=1, keepdims=True) + NORM_EPS)
            normed = (wide * scale).astype(jnp.bfloat16)
            for weight_ref, into in ((query_ref, q_rows), (key_ref, k_rows), (value_ref, v_rows)):
                made = by_rows(normed, weight_ref[...])
                into[0, at, :] = made[:, :128]
                into[1, at, :] = made[:, 128:]
            return carry

        lax.fori_loop(0, FRAMES // span, project, 0, unroll=True)

        def cell_rows(ref, cell):
            at = pl.ds(cell, FRAMES, stride=part)
            return jnp.concatenate([ref[0, at, :], ref[1, at, :]], axis=1).astype(jnp.bfloat16)

        def spread(found):
            zero = jnp.zeros_like(found)
            return jnp.concatenate([jnp.where(head_of == h, found, zero) for h in range(HEADS)], 0)

        def attend(cell, carry):
            queries = cell_rows(q_rows, cell)
            keys = spread(cell_rows(k_rows, cell))
            values = spread(cell_rows(v_rows, cell))
            scores = jnp.where(key_mask, by_rows(queries, keys), -1e30)
            tops = []
            for half in range(2):
                piece = scores[:, half * 128 : half * 128 + 128]
                low = jnp.max(jnp.where(low_half, piece, -1e30), axis=1, keepdims=True)
                high = jnp.max(jnp.where(low_half, -1e30, piece), axis=1, keepdims=True)
                tops.append(jnp.where(low_half, low, high))
            top = jnp.concatenate(tops, axis=1)
            weights = jnp.exp2((scores - top) * (LOG2_E * HD**-0.5)).astype(jnp.bfloat16)
            weighted = jnp.dot(weights, values, preferred_element_type=jnp.float32)
            sums = jnp.dot(weights, ones4, preferred_element_type=jnp.float32)
            attended = weighted / sums
            at = pl.ds(cell, FRAMES, stride=part)
            att_rows[0, at, :] = attended[:, :128]
            att_rows[1, at, :] = attended[:, 128:]
            return carry

        lax.fori_loop(0, part, attend, 0, unroll=True)

        def finish(b, carry, chunk=chunk):
            at = pl.ds(pl.multiple_of(b * block, block), block)
            attended = jnp.concatenate([att_rows[0, at, :], att_rows[1, at, :]], axis=1)
            full = residual[at, :].astype(jnp.float32) + by_rows(
                attended.astype(jnp.bfloat16), out_weight_ref[...]
            )
            frame = b * span + lax.broadcasted_iota(jnp.int32, (block, C2), 0) // part
            kept = jnp.where(frame < length, full, 0.0).astype(jnp.bfloat16)
            done_rows[chunk, pl.ds(b * span, span)] = kept.reshape(span, part, C2)
            wide = kept.astype(jnp.float32)
            squares = jnp.sum((wide * wide).reshape(block // 8, 8, C2), axis=0)
            total[...] += squares[:, :128] + squares[:, 128:]
            return carry

        lax.fori_loop(0, FRAMES // span, finish, 0, unroll=True)
        if chunk == CHUNKS - 1:
            each(1, count, lambda d: frame_sum(d).start())
            frame_sums[me] = total[...]
            each(1, HALF_WAY, lambda d, chunk=chunk: back(chunk, d).start())
            each(1, count, lambda d: frame_sum(d).wait_recv())
            group_total[...] = jnp.sum(frame_sums[...], axis=0)
            each(1, scenes, lambda d: scene_sum(d).start())
            scene_sums[my_scene] = group_total[...]
            each(HALF_WAY, count, lambda d, chunk=chunk: back(chunk, d).start())
        else:
            each(1, count, lambda d, chunk=chunk: back(chunk, d).start())
        returned[:, cells_of(me, chunk), :] = done_rows[chunk, pl.ds(f_dev * me, f_dev)]

    for chunk in range(CHUNKS):
        each(1, count, lambda d, chunk=chunk: back(chunk, d).wait_recv())

    for f in range(f_dev):
        encoded_ref[f] = returned[f].T

    each(1, scenes, lambda d: scene_sum(d).wait_recv())
    slots = float(scenes * FRAMES * CELLS * C2)
    loss_ref[...] = jnp.sum(jnp.sum(scene_sums[...], axis=0), keepdims=True) * (0.5 / slots)
    each(1, count, lambda d: frame_sum(d).wait_send())
    each(1, scenes, lambda d: scene_sum(d).wait_send())
    for piece in range(len(pieces)):
        each(1, count, lambda d, piece=piece: there(piece, d).wait_send())
    for chunk in range(CHUNKS):
        each(1, count, lambda d, chunk=chunk: back(chunk, d).wait_send())


def shards(
    occupancy,
    scene_lengths,
    conv1_weight,
    conv2_weight,
    temporal_weight,
    query_weight,
    key_weight,
    value_weight,
    out_weight,
):
    f_dev = occupancy.shape[1]
    count, scenes = lax.axis_size("frame"), lax.axis_size("scene")
    operands = (
        occupancy[0],
        jnp.asarray(picks_strided(), jnp.bfloat16),
        conv1_weight.T,
        conv2_weight,
        jnp.asarray(picks_near(), jnp.bfloat16),
        temporal_weight,
        query_weight,
        key_weight,
        value_weight,
        out_weight,
    )
    part = CELLS // count // CHUNKS
    rows = FRAMES * part
    wide_rows = pltpu.VMEM((2, rows, 128), jnp.float32)
    in_vmem = pl.BlockSpec(memory_space=pltpu.VMEM)
    encoded, loss = pl.pallas_call(
        functools.partial(mixing_kernel, count, scenes),
        out_shape=(
            jax.ShapeDtypeStruct((f_dev, C2, CELLS), jnp.bfloat16),
            jax.ShapeDtypeStruct((1, 1), jnp.float32),
        ),
        in_specs=[pl.BlockSpec(memory_space=pltpu.SMEM)] + [pl.BlockSpec(memory_space=pl.ANY)] * 10,
        out_specs=(in_vmem, in_vmem),
        scratch_shapes=[pltpu.VMEM(array.shape, array.dtype) for array in operands]
        + [
            pltpu.VMEM((CIN * 27, C1), jnp.float32),
            pltpu.VMEM((2, C1 * 27, 128), jnp.float32),
            pltpu.VMEM((3, 10 * CIN, C1), jnp.bfloat16),
            pltpu.VMEM((3, 9 * C1, C2), jnp.bfloat16),
            pltpu.VMEM((2, 8, 64, 10 * CIN), jnp.bfloat16),
            pltpu.VMEM((2, 9, 64, 10 * CIN), jnp.bfloat16),
            pltpu.VMEM((CELLS, 2 * C1), jnp.bfloat16),
            pltpu.VMEM((2, 10, 64, 9 * C1), jnp.bfloat16),
            pltpu.VMEM((f_dev, CELLS, C2), jnp.bfloat16),
            pltpu.VMEM((FRAMES + 2, CELLS // count, C2), jnp.bfloat16),
            pltpu.VMEM((rows, C2), jnp.bfloat16),
            wide_rows,
            wide_rows,
            wide_rows,
            wide_rows,
            pltpu.VMEM((CHUNKS, FRAMES, part, C2), jnp.bfloat16),
            pltpu.VMEM((f_dev, CELLS, C2), jnp.bfloat16),
            pltpu.VMEM((8, 128), jnp.float32),
            pltpu.VMEM((8, 128), jnp.float32),
            pltpu.VMEM((count, 8, 128), jnp.float32),
            pltpu.VMEM((scenes, 8, 128), jnp.float32),
        ]
        + [pltpu.SemaphoreType.DMA((CHUNKS + f_dev - 2, count))] * 2
        + [pltpu.SemaphoreType.DMA((CHUNKS, count))] * 2
        + [pltpu.SemaphoreType.DMA((count,))] * 2
        + [pltpu.SemaphoreType.DMA((scenes,))] * 2
        + [pltpu.SemaphoreType.DMA((10,))],
        compiler_params=pltpu.CompilerParams(
            collective_id=0, has_side_effects=True, vmem_limit_bytes=60 * 2**20
        ),
    )(scene_lengths, *operands)
    return (encoded[None], loss.reshape(()))


def solution(mesh):
    placed = (P("scene", "frame", None, None), P("scene"), P(), P(), P(), P(), P(), P(), P())
    return jax.shard_map(
        shards,
        mesh=mesh,
        in_specs=placed,
        out_specs=(P("scene", "frame", None, None), P()),
        check_vma=False,
    )
```

```python
import functools

import jax
import jax.numpy as jnp
import numpy as np
from jax import lax
from jax.experimental import pallas as pl
from jax.experimental.pallas import tpu as pltpu
from jax.sharding import PartitionSpec as P

CIN = 64
C1 = 128
C2 = 256
HEADS = 4
HD = 64
HI = 16
ZD = 8
CELLS = 512


NORM_EPS = 1e-06


FRAMES = 64
CHUNKS = 2
SIDE = 4
HALF_WAY = 8
OFFSETS = (
    (2, 2),
    (2, 1),
    (2, 3),
    (1, 2),
    (3, 2),
    (2, 0),
    (0, 2),
    (1, 1),
    (3, 3),
    (1, 3),
    (3, 1),
    (0, 1),
    (0, 3),
    (1, 0),
    (3, 0),
)
LOG2_E = 1.4426950408889634


def by_rows(rows, weight):
    return lax.dot_general(
        rows, weight, (((1,), (1,)), ((), ())), preferred_element_type=jnp.float32
    )


def by_columns(rows, matrix):
    return jnp.dot(rows, matrix, preferred_element_type=jnp.float32)


def silu(v):
    return 0.5 * v * (1.0 + jnp.tanh(0.5 * v))


def picks_strided():
    picks = np.zeros((5, 8, ZD, 2, HI, ZD), np.float32)
    for tap in range(9):
        for out_y in range(8):
            for out_z in range(ZD):
                y, z = 2 * out_y + tap // 3 - 1, out_z + tap % 3 - 1
                if 0 <= y < HI and 0 <= z < ZD:
                    picks[tap // 2, out_y, out_z, tap % 2, y, z] = 1
    return picks.reshape(5 * 64, 2 * HI * ZD)


def picks_near():
    picks = np.zeros((9, 8, ZD, 8, ZD), np.float32)
    for tap in range(9):
        for out_y in range(8):
            for out_z in range(ZD):
                y, z = out_y + tap // 3 - 1, out_z + tap % 3 - 1
                if 0 <= y < 8 and 0 <= z < ZD:
                    picks[tap, out_y, out_z, y, z] = 1
    return picks.reshape(9 * 64, 64)


def order_first(conv1_ref, tall1, taps1):
    tall1[...] = conv1_ref[...].astype(jnp.float32)
    for dx in range(3):
        for tap in range(9):
            at = pl.ds(dx * 9 + tap, CIN, stride=27)
            taps1[dx, tap * CIN : (tap + 1) * CIN, :] = tall1[at, :].astype(jnp.bfloat16)
        taps1[dx, 9 * CIN :, :] = jnp.zeros((CIN, C1), jnp.bfloat16)


def order_second(conv2_ref, tall2, taps2):
    eye = (
        lax.broadcasted_iota(jnp.int32, (128, 128), 0)
        == lax.broadcasted_iota(jnp.int32, (128, 128), 1)
    ).astype(jnp.bfloat16)
    for at in range(0, C1 * 27, 128):
        turned = by_rows(eye, conv2_ref[:, at : at + 128])
        tall2[0, at : at + 128, :] = turned[:, :128]
        tall2[1, at : at + 128, :] = turned[:, 128:]
    for dx in range(3):
        for tap in range(9):
            at = pl.ds(dx * 9 + tap, C1, stride=27)
            taps2[dx, tap * C1 : (tap + 1) * C1, :] = jnp.concatenate(
                [tall2[0, at, :], tall2[1, at, :]], axis=1
            ).astype(jnp.bfloat16)


def convolve_pair(
    pair, first_frame, length, ready, send, occupancy_ref, picks1, picks2, taps1, taps2, even, odd, maps, near, second
):
    blank = jnp.zeros((CIN, 128), jnp.bfloat16)
    for x in range(HI):
        pieces = []
        for f in range(2):
            plane = occupancy_ref[2 * pair + f, :, x * 128 : (x + 1) * 128]
            pieces.append(jnp.concatenate([plane, blank], axis=1))
            pieces.append(jnp.concatenate([blank, plane], axis=1))
        found = by_rows(picks1[...], jnp.concatenate(pieces, axis=0)).astype(jnp.bfloat16)
        into, row = (even, x // 2) if x % 2 == 0 else (odd, x // 2 + 1)
        for f in range(2):
            for k in range(5):
                into[f, row, :, k * 128 : (k + 1) * 128] = found[
                    k * 64 : (k + 1) * 64, f * 128 : (f + 1) * 128
                ]
    ready(1)
    for f in range(2):
        planes = [odd[f, 0:8], even[f], odd[f, 1:9]]
        planes = jnp.concatenate([p.reshape(CELLS, 10 * CIN) for p in planes], axis=1)
        total = by_columns(planes, taps1[...].reshape(30 * CIN, C1))
        maps[:, f * C1 : (f + 1) * C1] = silu(total).astype(jnp.bfloat16)
    ready(2)
    for x in range(8):
        found = by_columns(picks2[...], maps[x * 64 : (x + 1) * 64, :]).astype(jnp.bfloat16)
        for f in range(2):
            for k in range(9):
                near[f, x + 1, :, k * C1 : (k + 1) * C1] = found[
                    k * 64 : (k + 1) * 64, f * C1 : (f + 1) * C1
                ]
    for f in range(2):
        planes = [near[f, dx : dx + 8].reshape(CELLS, 9 * C1) for dx in range(3)]
        total = by_columns(jnp.concatenate(planes, axis=1), taps2[...].reshape(27 * C1, C2))
        kept = jnp.where(first_frame + 2 * pair + f < length, silu(total), 0.0)
        second[2 * pair + f] = kept.astype(jnp.bfloat16)
        send(2 * pair + f)


def mixing_kernel(
    count,
    scenes,
    length_ref,
    occupancy_in,
    picks1_in,
    conv1_in,
    conv2_in,
    picks2_in,
    temporal_in,
    query_in,
    key_in,
    value_in,
    out_weight_in,
    encoded_ref,
    loss_ref,
    occupancy_ref,
    picks1,
    conv1_ref,
    conv2_ref,
    picks2,
    temporal_ref,
    query_ref,
    key_ref,
    value_ref,
    out_weight_ref,
    tall1,
    tall2,
    taps1,
    taps2,
    even,
    odd,
    maps,
    near,
    second,
    gathered,
    residual,
    q_rows,
    k_rows,
    v_rows,
    att_rows,
    done_rows,
    returned,
    total,
    group_total,
    frame_sums,
    scene_sums,
    there_send,
    there_recv,
    back_send,
    back_recv,
    frame_send,
    frame_recv,
    scene_send,
    scene_recv,
    load_sem,
):
    f_dev = occupancy_ref.shape[0]
    pairs = f_dev // 2
    cells = CELLS // count
    part = cells // CHUNKS
    rows = FRAMES * part
    me = lax.axis_index("frame")
    my_scene = lax.axis_index("scene")
    length = length_ref[0]

    loads = [
        pltpu.make_async_copy(source, into, load_sem.at[i])
        for i, (source, into) in enumerate(
            (
                (occupancy_in, occupancy_ref),
                (picks1_in, picks1),
                (conv1_in, conv1_ref),
                (conv2_in, conv2_ref),
                (picks2_in, picks2),
                (temporal_in, temporal_ref),
                (query_in, query_ref),
                (key_in, key_ref),
                (value_in, value_ref),
                (out_weight_in, out_weight_ref),
            )
        )
    ]
    for load in loads:
        load.start()

    barrier = pltpu.get_barrier_semaphore()

    def greet_frame(d, carry):
        pl.semaphore_signal(
            barrier,
            inc=1,
            device_id={"frame": lax.rem(me + d, count)},
            device_id_type=pl.DeviceIdType.MESH,
        )
        return carry

    def greet_scene(d, carry):
        pl.semaphore_signal(
            barrier,
            inc=1,
            device_id={"scene": lax.rem(my_scene + d, scenes)},
            device_id_type=pl.DeviceIdType.MESH,
        )
        return carry

    lax.fori_loop(1, count, greet_frame, 0)
    lax.fori_loop(1, scenes, greet_scene, 0)

    def cells_of(device, chunk):
        return pl.ds(pl.multiple_of(device * cells + chunk * part, part), part)

    pieces = [(frame, 1, 0, cells) for frame in range(f_dev - 2)]
    pieces += [(f_dev - 2, 2, chunk * part, part) for chunk in range(CHUNKS)]

    def peer(d):
        down, across = OFFSETS[d - 1]
        return lax.rem(me // SIDE + down, SIDE) * SIDE + lax.rem(me + across, SIDE)

    def there(piece, d):
        frame, frames, first, size = pieces[piece]
        to = peer(d)
        return pltpu.make_async_remote_copy(
            src_ref=second.at[
                pl.ds(frame, frames), pl.ds(pl.multiple_of(to * cells + first, part), size), :
            ],
            dst_ref=gathered.at[pl.ds(1 + f_dev * me + frame, frames), pl.ds(first, size)],
            send_sem=there_send.at[piece, d],
            recv_sem=there_recv.at[piece, d],
            device_id={"frame": to},
            device_id_type=pl.DeviceIdType.MESH,
        )

    def back(chunk, d):
        to = peer(d)
        return pltpu.make_async_remote_copy(
            src_ref=done_rows.at[chunk, pl.ds(f_dev * to, f_dev)],
            dst_ref=returned.at[:, cells_of(me, chunk), :],
            send_sem=back_send.at[chunk, d],
            recv_sem=back_recv.at[chunk, d],
            device_id={"frame": to},
            device_id_type=pl.DeviceIdType.MESH,
        )

    def frame_sum(d):
        return pltpu.make_async_remote_copy(
            src_ref=total,
            dst_ref=frame_sums.at[me],
            send_sem=frame_send.at[d],
            recv_sem=frame_recv.at[d],
            device_id={"frame": peer(d)},
            device_id_type=pl.DeviceIdType.MESH,
        )

    def scene_sum(d):
        return pltpu.make_async_remote_copy(
            src_ref=group_total,
            dst_ref=scene_sums.at[my_scene],
            send_sem=scene_send.at[d],
            recv_sem=scene_recv.at[d],
            device_id={"scene": lax.rem(my_scene + d, scenes)},
            device_id_type=pl.DeviceIdType.MESH,
        )

    def each(first, last, act):
        for d in range(first, last):
            act(d)

    for load in loads[:2]:
        load.wait()

    def ready(stage):
        if stage == 1:
            loads[2].wait()
            order_first(conv1_ref, tall1, taps1)
        else:
            loads[3].wait()
            loads[4].wait()
            order_second(conv2_ref, tall2, taps2)

    def send(frame):
        if frame == 0:
            pl.semaphore_wait(barrier, count - 1 + scenes - 1)
        for piece in range(len(pieces)):
            if pieces[piece][0] + pieces[piece][1] == frame + 1:
                each(1, count, lambda d, piece=piece: there(piece, d).start())

    for f in range(2):
        odd[f, 0] = jnp.zeros((64, 10 * CIN), jnp.bfloat16)
        near[f, 0] = jnp.zeros((64, 9 * C1), jnp.bfloat16)
        near[f, 9] = jnp.zeros((64, 9 * C1), jnp.bfloat16)
    gathered[0] = jnp.zeros((cells, C2), jnp.bfloat16)
    gathered[FRAMES + 1] = jnp.zeros((cells, C2), jnp.bfloat16)
    for pair in range(pairs):
        convolve_pair(
            pair,
            f_dev * me,
            length,
            ready if pair == 0 else lambda stage: None,
            send,
            occupancy_ref,
            picks1,
            picks2,
            taps1,
            taps2,
            even,
            odd,
            maps,
            near,
            second,
        )
    gathered[pl.ds(1 + f_dev * me, f_dev)] = second[
        :, pl.ds(pl.multiple_of(me * cells, cells), cells), :
    ]

    for load in loads[5:]:
        load.wait()

    span = 256 // part
    block = span * part
    head_of = lax.broadcasted_iota(jnp.int32, (FRAMES, C2), 1) // HD
    ones4 = (
        lax.broadcasted_iota(jnp.int32, (C2, C2), 0) // HD
        == lax.broadcasted_iota(jnp.int32, (C2, C2), 1) // HD
    ).astype(jnp.bfloat16)
    key_mask = lax.broadcasted_iota(jnp.int32, (FRAMES, C2), 1) % FRAMES < length
    low_half = lax.broadcasted_iota(jnp.int32, (FRAMES, 128), 1) < HD
    total[...] = jnp.zeros_like(total)

    for chunk in range(CHUNKS):
        for piece in range(len(pieces)):
            if pieces[piece][2] == chunk * part:
                each(1, count, lambda d, piece=piece: there(piece, d).wait_recv())

        def project(b, carry, chunk=chunk):
            window = gathered[pl.ds(b * span, span + 2), chunk * part : (chunk + 1) * part]
            window = window.reshape((span + 2) * part, C2)
            temporal = by_rows(window[:block], temporal_ref[0])
            temporal = temporal + by_rows(window[part : part + block], temporal_ref[1])
            temporal = temporal + by_rows(window[2 * part :], temporal_ref[2])
            here = window[part : part + block].astype(jnp.float32)
            mixed = (here + silu(temporal)).astype(jnp.bfloat16)
            at = pl.ds(pl.multiple_of(b * block, block), block)
            residual[at, :] = mixed
            wide = mixed.astype(jnp.float32)
            scale = lax.rsqrt(jnp.mean(wide * wide, axis=1, keepdims=True) + NORM_EPS)
            normed = (wide * scale).astype(jnp.bfloat16)
            for weight_ref, into in ((query_ref, q_rows), (key_ref, k_rows), (value_ref, v_rows)):
                made = by_rows(normed, weight_ref[...])
                into[0, at, :] = made[:, :128]
                into[1, at, :] = made[:, 128:]
            return carry

        lax.fori_loop(0, FRAMES // span, project, 0, unroll=True)

        def cell_rows(ref, cell):
            at = pl.ds(cell, FRAMES, stride=part)
            return jnp.concatenate([ref[0, at, :], ref[1, at, :]], axis=1).astype(jnp.bfloat16)

        def spread(found):
            zero = jnp.zeros_like(found)
            return jnp.concatenate([jnp.where(head_of == h, found, zero) for h in range(HEADS)], 0)

        def attend(cell, carry):
            queries = cell_rows(q_rows, cell)
            keys = spread(cell_rows(k_rows, cell))
            values = spread(cell_rows(v_rows, cell))
            scores = jnp.where(key_mask, by_rows(queries, keys), -1e30)
            tops = []
            for half in range(2):
                piece = scores[:, half * 128 : half * 128 + 128]
                low = jnp.max(jnp.where(low_half, piece, -1e30), axis=1, keepdims=True)
                high = jnp.max(jnp.where(low_half, -1e30, piece), axis=1, keepdims=True)
                tops.append(jnp.where(low_half, low, high))
            top = jnp.concatenate(tops, axis=1)
            weights = jnp.exp2((scores - top) * (LOG2_E * HD**-0.5)).astype(jnp.bfloat16)
            weighted = jnp.dot(weights, values, preferred_element_type=jnp.float32)
            sums = jnp.dot(weights, ones4, preferred_element_type=jnp.float32)
            attended = weighted / sums
            at = pl.ds(cell, FRAMES, stride=part)
            att_rows[0, at, :] = attended[:, :128]
            att_rows[1, at, :] = attended[:, 128:]
            return carry

        lax.fori_loop(0, part, attend, 0, unroll=True)

        def finish(b, carry, chunk=chunk):
            at = pl.ds(pl.multiple_of(b * block, block), block)
            attended = jnp.concatenate([att_rows[0, at, :], att_rows[1, at, :]], axis=1)
            full = residual[at, :].astype(jnp.float32) + by_rows(
                attended.astype(jnp.bfloat16), out_weight_ref[...]
            )
            frame = b * span + lax.broadcasted_iota(jnp.int32, (block, C2), 0) // part
            kept = jnp.where(frame < length, full, 0.0).astype(jnp.bfloat16)
            done_rows[chunk, pl.ds(b * span, span)] = kept.reshape(span, part, C2)
            wide = kept.astype(jnp.float32)
            squares = jnp.sum((wide * wide).reshape(block // 8, 8, C2), axis=0)
            total[...] += squares[:, :128] + squares[:, 128:]
            return carry

        lax.fori_loop(0, FRAMES // span, finish, 0, unroll=True)
        if chunk == CHUNKS - 1:
            each(1, count, lambda d: frame_sum(d).start())
            frame_sums[me] = total[...]
            each(1, HALF_WAY, lambda d, chunk=chunk: back(chunk, d).start())
            each(1, count, lambda d: frame_sum(d).wait_recv())
            group_total[...] = jnp.sum(frame_sums[...], axis=0)
            each(1, scenes, lambda d: scene_sum(d).start())
            scene_sums[my_scene] = group_total[...]
            each(HALF_WAY, count, lambda d, chunk=chunk: back(chunk, d).start())
        else:
            each(1, count, lambda d, chunk=chunk: back(chunk, d).start())
        returned[:, cells_of(me, chunk), :] = done_rows[chunk, pl.ds(f_dev * me, f_dev)]

    for down in (2, 1, 3, 0):
        for d in range(1, count):
            if OFFSETS[d - 1][0] == down:
                for chunk in range(CHUNKS):
                    back(chunk, d).wait_recv()
        row = lax.rem(me // SIDE + SIDE - down, SIDE)
        tile = pl.ds(pl.multiple_of(row * SIDE * cells, SIDE * cells), SIDE * cells)
        for f in range(f_dev):
            encoded_ref[f, :, tile] = returned[f, tile, :].T

    each(1, scenes, lambda d: scene_sum(d).wait_recv())
    slots = float(scenes * FRAMES * CELLS * C2)
    loss_ref[...] = jnp.sum(jnp.sum(scene_sums[...], axis=0), keepdims=True) * (0.5 / slots)
    each(1, count, lambda d: frame_sum(d).wait_send())
    each(1, scenes, lambda d: scene_sum(d).wait_send())
    for piece in range(len(pieces)):
        each(1, count, lambda d, piece=piece: there(piece, d).wait_send())
    for chunk in range(CHUNKS):
        each(1, count, lambda d, chunk=chunk: back(chunk, d).wait_send())


def shards(
    occupancy,
    scene_lengths,
    conv1_weight,
    conv2_weight,
    temporal_weight,
    query_weight,
    key_weight,
    value_weight,
    out_weight,
):
    f_dev = occupancy.shape[1]
    count, scenes = lax.axis_size("frame"), lax.axis_size("scene")
    operands = (
        occupancy[0],
        jnp.asarray(picks_strided(), jnp.bfloat16),
        conv1_weight.T,
        conv2_weight,
        jnp.asarray(picks_near(), jnp.bfloat16),
        temporal_weight,
        query_weight,
        key_weight,
        value_weight,
        out_weight,
    )
    part = CELLS // count // CHUNKS
    rows = FRAMES * part
    wide_rows = pltpu.VMEM((2, rows, 128), jnp.float32)
    in_vmem = pl.BlockSpec(memory_space=pltpu.VMEM)
    encoded, loss = pl.pallas_call(
        functools.partial(mixing_kernel, count, scenes),
        out_shape=(
            pltpu.VMEM((f_dev, C2, CELLS), jnp.bfloat16),
            pltpu.VMEM((1, 1), jnp.float32),
        ),
        in_specs=[pl.BlockSpec(memory_space=pltpu.SMEM)] + [pl.BlockSpec(memory_space=pl.ANY)] * 10,
        out_specs=(in_vmem, in_vmem),
        scratch_shapes=[pltpu.VMEM(array.shape, array.dtype) for array in operands]
        + [
            pltpu.VMEM((CIN * 27, C1), jnp.float32),
            pltpu.VMEM((2, C1 * 27, 128), jnp.float32),
            pltpu.VMEM((3, 10 * CIN, C1), jnp.bfloat16),
            pltpu.VMEM((3, 9 * C1, C2), jnp.bfloat16),
            pltpu.VMEM((2, 8, 64, 10 * CIN), jnp.bfloat16),
            pltpu.VMEM((2, 9, 64, 10 * CIN), jnp.bfloat16),
            pltpu.VMEM((CELLS, 2 * C1), jnp.bfloat16),
            pltpu.VMEM((2, 10, 64, 9 * C1), jnp.bfloat16),
            pltpu.VMEM((f_dev, CELLS, C2), jnp.bfloat16),
            pltpu.VMEM((FRAMES + 2, CELLS // count, C2), jnp.bfloat16),
            pltpu.VMEM((rows, C2), jnp.bfloat16),
            wide_rows,
            wide_rows,
            wide_rows,
            wide_rows,
            pltpu.VMEM((CHUNKS, FRAMES, part, C2), jnp.bfloat16),
            pltpu.VMEM((f_dev, CELLS, C2), jnp.bfloat16),
            pltpu.VMEM((8, 128), jnp.float32),
            pltpu.VMEM((8, 128), jnp.float32),
            pltpu.VMEM((count, 8, 128), jnp.float32),
            pltpu.VMEM((scenes, 8, 128), jnp.float32),
        ]
        + [pltpu.SemaphoreType.DMA((CHUNKS + f_dev - 2, count))] * 2
        + [pltpu.SemaphoreType.DMA((CHUNKS, count))] * 2
        + [pltpu.SemaphoreType.DMA((count,))] * 2
        + [pltpu.SemaphoreType.DMA((scenes,))] * 2
        + [pltpu.SemaphoreType.DMA((10,))],
        compiler_params=pltpu.CompilerParams(
            collective_id=0, has_side_effects=True, vmem_limit_bytes=60 * 2**20
        ),
    )(scene_lengths, *operands)
    return (encoded[None], loss.reshape(()))


def solution(mesh):
    placed = (P("scene", "frame", None, None), P("scene"), P(), P(), P(), P(), P(), P(), P())
    return jax.shard_map(
        shards,
        mesh=mesh,
        in_specs=placed,
        out_specs=(P("scene", "frame", None, None), P()),
        check_vma=False,
    )
```

```python
import functools

import jax
import jax.numpy as jnp
import numpy as np
from jax import lax
from jax.experimental import pallas as pl
from jax.experimental.pallas import tpu as pltpu
from jax.sharding import PartitionSpec as P

CIN = 64
C1 = 128
C2 = 256
HEADS = 4
HD = 64
HI = 16
ZD = 8
CELLS = 512


NORM_EPS = 1e-06


FRAMES = 64
CHUNKS = 2
SIDE = 4
HALF_WAY = 5
OFFSETS = (
    (2, 2),
    (2, 1),
    (2, 3),
    (1, 2),
    (3, 2),
    (2, 0),
    (0, 2),
    (1, 1),
    (3, 3),
    (1, 3),
    (3, 1),
    (0, 1),
    (0, 3),
    (1, 0),
    (3, 0),
)
LOG2_E = 1.4426950408889634


def by_rows(rows, weight):
    return lax.dot_general(
        rows, weight, (((1,), (1,)), ((), ())), preferred_element_type=jnp.float32
    )


def by_columns(rows, matrix):
    return jnp.dot(rows, matrix, preferred_element_type=jnp.float32)


def silu(v):
    return 0.5 * v * (1.0 + jnp.tanh(0.5 * v))


def picks_strided():
    picks = np.zeros((5, 8, ZD, 2, HI, ZD), np.float32)
    for tap in range(9):
        for out_y in range(8):
            for out_z in range(ZD):
                y, z = 2 * out_y + tap // 3 - 1, out_z + tap % 3 - 1
                if 0 <= y < HI and 0 <= z < ZD:
                    picks[tap // 2, out_y, out_z, tap % 2, y, z] = 1
    return picks.reshape(5 * 64, 2 * HI * ZD)


def picks_near():
    picks = np.zeros((9, 8, ZD, 8, ZD), np.float32)
    for tap in range(9):
        for out_y in range(8):
            for out_z in range(ZD):
                y, z = out_y + tap // 3 - 1, out_z + tap % 3 - 1
                if 0 <= y < 8 and 0 <= z < ZD:
                    picks[tap, out_y, out_z, y, z] = 1
    return picks.reshape(9 * 64, 64)


def order_first(conv1_ref, tall1, taps1):
    tall1[...] = conv1_ref[...].astype(jnp.float32)
    for dx in range(3):
        for tap in range(9):
            at = pl.ds(dx * 9 + tap, CIN, stride=27)
            taps1[dx, tap * CIN : (tap + 1) * CIN, :] = tall1[at, :].astype(jnp.bfloat16)
        taps1[dx, 9 * CIN :, :] = jnp.zeros((CIN, C1), jnp.bfloat16)


def order_second(conv2_ref, tall2, taps2):
    eye = (
        lax.broadcasted_iota(jnp.int32, (128, 128), 0)
        == lax.broadcasted_iota(jnp.int32, (128, 128), 1)
    ).astype(jnp.bfloat16)
    for at in range(0, C1 * 27, 128):
        turned = by_rows(eye, conv2_ref[:, at : at + 128])
        tall2[0, at : at + 128, :] = turned[:, :128]
        tall2[1, at : at + 128, :] = turned[:, 128:]
    for dx in range(3):
        for tap in range(9):
            at = pl.ds(dx * 9 + tap, C1, stride=27)
            taps2[dx, tap * C1 : (tap + 1) * C1, :] = jnp.concatenate(
                [tall2[0, at, :], tall2[1, at, :]], axis=1
            ).astype(jnp.bfloat16)


def convolve_pair(
    pair, first_frame, length, ready, send, occupancy_ref, picks1, picks2, taps1, taps2, even, odd, maps, near, second
):
    blank = jnp.zeros((CIN, 128), jnp.bfloat16)
    for x in range(HI):
        pieces = []
        for f in range(2):
            plane = occupancy_ref[2 * pair + f, :, x * 128 : (x + 1) * 128]
            pieces.append(jnp.concatenate([plane, blank], axis=1))
            pieces.append(jnp.concatenate([blank, plane], axis=1))
        found = by_rows(picks1[...], jnp.concatenate(pieces, axis=0)).astype(jnp.bfloat16)
        into, row = (even, x // 2) if x % 2 == 0 else (odd, x // 2 + 1)
        for f in range(2):
            for k in range(5):
                into[f, row, :, k * 128 : (k + 1) * 128] = found[
                    k * 64 : (k + 1) * 64, f * 128 : (f + 1) * 128
                ]
    ready(1)
    for f in range(2):
        planes = [odd[f, 0:8], even[f], odd[f, 1:9]]
        planes = jnp.concatenate([p.reshape(CELLS, 10 * CIN) for p in planes], axis=1)
        total = by_columns(planes, taps1[...].reshape(30 * CIN, C1))
        maps[:, f * C1 : (f + 1) * C1] = silu(total).astype(jnp.bfloat16)
    ready(2)
    for x in range(8):
        found = by_columns(picks2[...], maps[x * 64 : (x + 1) * 64, :]).astype(jnp.bfloat16)
        for f in range(2):
            for k in range(9):
                near[f, x + 1, :, k * C1 : (k + 1) * C1] = found[
                    k * 64 : (k + 1) * 64, f * C1 : (f + 1) * C1
                ]
    for f in range(2):
        planes = [near[f, dx : dx + 8].reshape(CELLS, 9 * C1) for dx in range(3)]
        total = by_columns(jnp.concatenate(planes, axis=1), taps2[...].reshape(27 * C1, C2))
        kept = jnp.where(first_frame + 2 * pair + f < length, silu(total), 0.0)
        second[2 * pair + f] = kept.astype(jnp.bfloat16)
        send(2 * pair + f)


def mixing_kernel(
    count,
    scenes,
    length_ref,
    occupancy_in,
    picks1_in,
    conv1_in,
    conv2_in,
    picks2_in,
    temporal_in,
    query_in,
    key_in,
    value_in,
    out_weight_in,
    encoded_ref,
    loss_ref,
    occupancy_ref,
    picks1,
    conv1_ref,
    conv2_ref,
    picks2,
    temporal_ref,
    query_ref,
    key_ref,
    value_ref,
    out_weight_ref,
    tall1,
    tall2,
    taps1,
    taps2,
    even,
    odd,
    maps,
    near,
    second,
    gathered,
    residual,
    q_rows,
    k_rows,
    v_rows,
    att_rows,
    done_rows,
    returned,
    total,
    group_total,
    frame_sums,
    scene_sums,
    there_send,
    there_recv,
    back_send,
    back_recv,
    frame_send,
    frame_recv,
    scene_send,
    scene_recv,
    load_sem,
):
    f_dev = occupancy_ref.shape[0]
    pairs = f_dev // 2
    cells = CELLS // count
    part = cells // CHUNKS
    rows = FRAMES * part
    me = lax.axis_index("frame")
    my_scene = lax.axis_index("scene")
    length = length_ref[0]

    loads = [
        pltpu.make_async_copy(source, into, load_sem.at[i])
        for i, (source, into) in enumerate(
            (
                (occupancy_in, occupancy_ref),
                (picks1_in, picks1),
                (conv1_in, conv1_ref),
                (conv2_in, conv2_ref),
                (picks2_in, picks2),
                (temporal_in, temporal_ref),
                (query_in, query_ref),
                (key_in, key_ref),
                (value_in, value_ref),
                (out_weight_in, out_weight_ref),
            )
        )
    ]
    for load in loads:
        load.start()

    barrier = pltpu.get_barrier_semaphore()

    def greet_frame(d, carry):
        pl.semaphore_signal(
            barrier,
            inc=1,
            device_id={"frame": lax.rem(me + d, count)},
            device_id_type=pl.DeviceIdType.MESH,
        )
        return carry

    def greet_scene(d, carry):
        pl.semaphore_signal(
            barrier,
            inc=1,
            device_id={"scene": lax.rem(my_scene + d, scenes)},
            device_id_type=pl.DeviceIdType.MESH,
        )
        return carry

    lax.fori_loop(1, count, greet_frame, 0)
    lax.fori_loop(1, scenes, greet_scene, 0)

    def cells_of(device, chunk):
        return pl.ds(pl.multiple_of(device * cells + chunk * part, part), part)

    pieces = [(frame, 1, 0, cells) for frame in range(f_dev - 2)]
    pieces += [(f_dev - 2, 2, chunk * part, part) for chunk in range(CHUNKS)]

    def peer(d):
        down, across = OFFSETS[d - 1]
        return lax.rem(me // SIDE + down, SIDE) * SIDE + lax.rem(me + across, SIDE)

    def there(piece, d):
        frame, frames, first, size = pieces[piece]
        to = peer(d)
        return pltpu.make_async_remote_copy(
            src_ref=second.at[
                pl.ds(frame, frames), pl.ds(pl.multiple_of(to * cells + first, part), size), :
            ],
            dst_ref=gathered.at[pl.ds(1 + f_dev * me + frame, frames), pl.ds(first, size)],
            send_sem=there_send.at[piece, d],
            recv_sem=there_recv.at[piece, d],
            device_id={"frame": to},
            device_id_type=pl.DeviceIdType.MESH,
        )

    def back(chunk, d):
        to = peer(d)
        return pltpu.make_async_remote_copy(
            src_ref=done_rows.at[chunk, pl.ds(f_dev * to, f_dev)],
            dst_ref=returned.at[chunk, me],
            send_sem=back_send.at[chunk, d],
            recv_sem=back_recv.at[chunk, d],
            device_id={"frame": to},
            device_id_type=pl.DeviceIdType.MESH,
        )

    def frame_sum(d):
        return pltpu.make_async_remote_copy(
            src_ref=total,
            dst_ref=frame_sums.at[me],
            send_sem=frame_send.at[d],
            recv_sem=frame_recv.at[d],
            device_id={"frame": peer(d)},
            device_id_type=pl.DeviceIdType.MESH,
        )

    def scene_sum(d):
        return pltpu.make_async_remote_copy(
            src_ref=group_total,
            dst_ref=scene_sums.at[my_scene],
            send_sem=scene_send.at[d],
            recv_sem=scene_recv.at[d],
            device_id={"scene": lax.rem(my_scene + d, scenes)},
            device_id_type=pl.DeviceIdType.MESH,
        )

    def each(first, last, act):
        for d in range(first, last):
            act(d)

    for load in loads[:2]:
        load.wait()

    def ready(stage):
        if stage == 1:
            loads[2].wait()
            order_first(conv1_ref, tall1, taps1)
        else:
            loads[3].wait()
            loads[4].wait()
            order_second(conv2_ref, tall2, taps2)

    def send(frame):
        if frame == 0:
            pl.semaphore_wait(barrier, count - 1 + scenes - 1)
        for piece in range(len(pieces)):
            if pieces[piece][0] + pieces[piece][1] == frame + 1:
                each(1, count, lambda d, piece=piece: there(piece, d).start())

    for f in range(2):
        odd[f, 0] = jnp.zeros((64, 10 * CIN), jnp.bfloat16)
        near[f, 0] = jnp.zeros((64, 9 * C1), jnp.bfloat16)
        near[f, 9] = jnp.zeros((64, 9 * C1), jnp.bfloat16)
    gathered[0] = jnp.zeros((cells, C2), jnp.bfloat16)
    gathered[FRAMES + 1] = jnp.zeros((cells, C2), jnp.bfloat16)
    for pair in range(pairs):
        convolve_pair(
            pair,
            f_dev * me,
            length,
            ready if pair == 0 else lambda stage: None,
            send,
            occupancy_ref,
            picks1,
            picks2,
            taps1,
            taps2,
            even,
            odd,
            maps,
            near,
            second,
        )
    gathered[pl.ds(1 + f_dev * me, f_dev)] = second[
        :, pl.ds(pl.multiple_of(me * cells, cells), cells), :
    ]

    for load in loads[5:]:
        load.wait()

    span = 256 // part
    block = span * part
    head_of = lax.broadcasted_iota(jnp.int32, (FRAMES, C2), 1) // HD
    ones4 = (
        lax.broadcasted_iota(jnp.int32, (C2, C2), 0) // HD
        == lax.broadcasted_iota(jnp.int32, (C2, C2), 1) // HD
    ).astype(jnp.bfloat16)
    key_mask = lax.broadcasted_iota(jnp.int32, (FRAMES, C2), 1) % FRAMES < length
    low_half = lax.broadcasted_iota(jnp.int32, (FRAMES, 128), 1) < HD
    total[...] = jnp.zeros_like(total)

    for chunk in range(CHUNKS):
        for piece in range(len(pieces)):
            if pieces[piece][2] == chunk * part:
                each(1, count, lambda d, piece=piece: there(piece, d).wait_recv())

        def project(b, carry, chunk=chunk):
            window = gathered[pl.ds(b * span, span + 2), chunk * part : (chunk + 1) * part]
            window = window.reshape((span + 2) * part, C2)
            temporal = by_rows(window[:block], temporal_ref[0])
            temporal = temporal + by_rows(window[part : part + block], temporal_ref[1])
            temporal = temporal + by_rows(window[2 * part :], temporal_ref[2])
            here = window[part : part + block].astype(jnp.float32)
            mixed = (here + silu(temporal)).astype(jnp.bfloat16)
            at = pl.ds(pl.multiple_of(b * block, block), block)
            residual[at, :] = mixed
            wide = mixed.astype(jnp.float32)
            scale = lax.rsqrt(jnp.mean(wide * wide, axis=1, keepdims=True) + NORM_EPS)
            normed = (wide * scale).astype(jnp.bfloat16)
            for weight_ref, into in ((query_ref, q_rows), (key_ref, k_rows), (value_ref, v_rows)):
                made = by_rows(normed, weight_ref[...])
                into[0, at, :] = made[:, :128]
                into[1, at, :] = made[:, 128:]
            return carry

        lax.fori_loop(0, FRAMES // span, project, 0, unroll=True)

        def cell_rows(ref, cell):
            at = pl.ds(cell, FRAMES, stride=part)
            return jnp.concatenate([ref[0, at, :], ref[1, at, :]], axis=1).astype(jnp.bfloat16)

        def spread(found):
            zero = jnp.zeros_like(found)
            return jnp.concatenate([jnp.where(head_of == h, found, zero) for h in range(HEADS)], 0)

        def attend(cell, carry):
            queries = cell_rows(q_rows, cell)
            keys = spread(cell_rows(k_rows, cell))
            values = spread(cell_rows(v_rows, cell))
            scores = jnp.where(key_mask, by_rows(queries, keys), -1e30)
            tops = []
            for half in range(2):
                piece = scores[:, half * 128 : half * 128 + 128]
                low = jnp.max(jnp.where(low_half, piece, -1e30), axis=1, keepdims=True)
                high = jnp.max(jnp.where(low_half, -1e30, piece), axis=1, keepdims=True)
                tops.append(jnp.where(low_half, low, high))
            top = jnp.concatenate(tops, axis=1)
            weights = jnp.exp2((scores - top) * (LOG2_E * HD**-0.5)).astype(jnp.bfloat16)
            weighted = jnp.dot(weights, values, preferred_element_type=jnp.float32)
            sums = jnp.dot(weights, ones4, preferred_element_type=jnp.float32)
            attended = weighted / sums
            at = pl.ds(cell, FRAMES, stride=part)
            att_rows[0, at, :] = attended[:, :128]
            att_rows[1, at, :] = attended[:, 128:]
            return carry

        lax.fori_loop(0, part, attend, 0, unroll=True)

        def finish(b, carry, chunk=chunk):
            at = pl.ds(pl.multiple_of(b * block, block), block)
            attended = jnp.concatenate([att_rows[0, at, :], att_rows[1, at, :]], axis=1)
            full = residual[at, :].astype(jnp.float32) + by_rows(
                attended.astype(jnp.bfloat16), out_weight_ref[...]
            )
            frame = b * span + lax.broadcasted_iota(jnp.int32, (block, C2), 0) // part
            kept = jnp.where(frame < length, full, 0.0).astype(jnp.bfloat16)
            done_rows[chunk, pl.ds(b * span, span)] = kept.reshape(span, part, C2)
            wide = kept.astype(jnp.float32)
            squares = jnp.sum((wide * wide).reshape(block // 8, 8, C2), axis=0)
            total[...] += squares[:, :128] + squares[:, 128:]
            return carry

        lax.fori_loop(0, FRAMES // span, finish, 0, unroll=True)
        if chunk == CHUNKS - 1:
            each(1, count, lambda d: frame_sum(d).start())
            frame_sums[me] = total[...]
            each(1, HALF_WAY, lambda d, chunk=chunk: back(chunk, d).start())
            each(1, count, lambda d: frame_sum(d).wait_recv())
            group_total[...] = jnp.sum(frame_sums[...], axis=0)
            each(1, scenes, lambda d: scene_sum(d).start())
            scene_sums[my_scene] = group_total[...]
            each(HALF_WAY, count, lambda d, chunk=chunk: back(chunk, d).start())
        else:
            each(1, count, lambda d, chunk=chunk: back(chunk, d).start())
        returned[chunk, me] = done_rows[chunk, pl.ds(f_dev * me, f_dev)]

    for piece in range(len(pieces)):
        each(1, count, lambda d, piece=piece: there(piece, d).wait_send())
    each(1, count, lambda d: frame_sum(d).wait_send())
    each(1, scenes, lambda d: scene_sum(d).wait_send())
    for chunk in range(CHUNKS - 1):
        each(1, count, lambda d, chunk=chunk: back(chunk, d).wait_send())
    for down in (2, 1, 3, 0):
        if down == 0:
            each(1, count, lambda d: back(CHUNKS - 1, d).wait_send())
        for d in range(1, count):
            if OFFSETS[d - 1][0] == down:
                for chunk in range(CHUNKS):
                    back(chunk, d).wait_recv()
        row = lax.rem(me // SIDE + SIDE - down, SIDE)
        tile = pl.ds(pl.multiple_of(row * SIDE * cells, SIDE * cells), SIDE * cells)
        for f in range(f_dev):
            found = [
                returned[chunk, row * SIDE + across, f]
                for across in range(SIDE)
                for chunk in range(CHUNKS)
            ]
            encoded_ref[f, :, tile] = jnp.concatenate(found, axis=0).T

    each(1, scenes, lambda d: scene_sum(d).wait_recv())
    slots = float(scenes * FRAMES * CELLS * C2)
    loss_ref[...] = jnp.sum(jnp.sum(scene_sums[...], axis=0), keepdims=True) * (0.5 / slots)


def shards(
    occupancy,
    scene_lengths,
    conv1_weight,
    conv2_weight,
    temporal_weight,
    query_weight,
    key_weight,
    value_weight,
    out_weight,
):
    f_dev = occupancy.shape[1]
    count, scenes = lax.axis_size("frame"), lax.axis_size("scene")
    operands = (
        occupancy[0],
        jnp.asarray(picks_strided(), jnp.bfloat16),
        conv1_weight.T,
        conv2_weight,
        jnp.asarray(picks_near(), jnp.bfloat16),
        temporal_weight,
        query_weight,
        key_weight,
        value_weight,
        out_weight,
    )
    part = CELLS // count // CHUNKS
    rows = FRAMES * part
    wide_rows = pltpu.VMEM((2, rows, 128), jnp.float32)
    in_vmem = pl.BlockSpec(memory_space=pltpu.VMEM)
    encoded, loss = pl.pallas_call(
        functools.partial(mixing_kernel, count, scenes),
        out_shape=(
            pltpu.VMEM((f_dev, C2, CELLS), jnp.bfloat16),
            pltpu.VMEM((1, 1), jnp.float32),
        ),
        in_specs=[pl.BlockSpec(memory_space=pltpu.SMEM)] + [pl.BlockSpec(memory_space=pl.ANY)] * 10,
        out_specs=(in_vmem, in_vmem),
        scratch_shapes=[pltpu.VMEM(array.shape, array.dtype) for array in operands]
        + [
            pltpu.VMEM((CIN * 27, C1), jnp.float32),
            pltpu.VMEM((2, C1 * 27, 128), jnp.float32),
            pltpu.VMEM((3, 10 * CIN, C1), jnp.bfloat16),
            pltpu.VMEM((3, 9 * C1, C2), jnp.bfloat16),
            pltpu.VMEM((2, 8, 64, 10 * CIN), jnp.bfloat16),
            pltpu.VMEM((2, 9, 64, 10 * CIN), jnp.bfloat16),
            pltpu.VMEM((CELLS, 2 * C1), jnp.bfloat16),
            pltpu.VMEM((2, 10, 64, 9 * C1), jnp.bfloat16),
            pltpu.VMEM((f_dev, CELLS, C2), jnp.bfloat16),
            pltpu.VMEM((FRAMES + 2, CELLS // count, C2), jnp.bfloat16),
            pltpu.VMEM((rows, C2), jnp.bfloat16),
            wide_rows,
            wide_rows,
            wide_rows,
            wide_rows,
            pltpu.VMEM((CHUNKS, FRAMES, part, C2), jnp.bfloat16),
            pltpu.VMEM((CHUNKS, count, f_dev, part, C2), jnp.bfloat16),
            pltpu.VMEM((8, 128), jnp.float32),
            pltpu.VMEM((8, 128), jnp.float32),
            pltpu.VMEM((count, 8, 128), jnp.float32),
            pltpu.VMEM((scenes, 8, 128), jnp.float32),
        ]
        + [pltpu.SemaphoreType.DMA((CHUNKS + f_dev - 2, count))] * 2
        + [pltpu.SemaphoreType.DMA((CHUNKS, count))] * 2
        + [pltpu.SemaphoreType.DMA((count,))] * 2
        + [pltpu.SemaphoreType.DMA((scenes,))] * 2
        + [pltpu.SemaphoreType.DMA((10,))],
        compiler_params=pltpu.CompilerParams(
            collective_id=0, has_side_effects=True, vmem_limit_bytes=60 * 2**20
        ),
    )(scene_lengths, *operands)
    return (encoded[None], loss.reshape(()))


def solution(mesh):
    placed = (P("scene", "frame", None, None), P("scene"), P(), P(), P(), P(), P(), P(), P())
    return jax.shard_map(
        shards,
        mesh=mesh,
        in_specs=placed,
        out_specs=(P("scene", "frame", None, None), P()),
        check_vma=False,
    )
```
